128 devices in a mesh: dp: 16 (over z, y), frame: 8 (over x, core).
Axes of the slice: x: 4, y: 4, z: 4, core: 2. Of those that a mesh axis runs over, the one named last changes fastest.
Arguments:
- frames: bfloat16 [2048, 8, 768], P('dp', 'frame'), may hold values from -34 to 34
- frame_gain: float32 [768], replicated, may hold values from 0.25 to 1.75
- w_up: bfloat16 [768, 3072], replicated, may hold values from -0.21875 to 0.21875
- w_down: bfloat16 [3072, 768], replicated, may hold values from -0.109375 to 0.109375
- pool_query: float32 [768], replicated, may hold values from -4 to 4
- pos_embed: bfloat16 [50, 768], replicated, may hold values from -5 to 5
- user_gain: float32 [768], replicated, may hold values from 0.25 to 1.75
- w_qkv: bfloat16 [768, 2304], replicated, may hold values from -0.7577722 to 0.7577722
- w_out: bfloat16 [768, 768], replicated, may hold values from -0.21875 to 0.21875
- request_rows: int32 [128, 16, 64], P(('dp', 'frame')), may hold values from -1 to 127, as said below
- hist_slot: int32 [2048, 50], P(('dp', 'frame')), may hold values from 0 to 1023, as said below
- hist_len: int32 [2048], P(('dp', 'frame')), may hold values from 1 to 50
- d_encoded: bfloat16 [2048, 50, 768], P(('dp', 'frame')), may hold values from -6 to 6
Outputs:
- encoded: bfloat16 [2048, 50, 768], P(('dp', 'frame'))
- d_frames: bfloat16 [2048, 8, 768], P('dp', 'frame')
The draws below stay inside these ranges and needn't reach their ends.
Inputs may be any that keep to these rules, and one draw needn't show every extreme that they name: `request_rows`: in each list of 64 entries the first ones are distinct local rows of that owner and the rest are -1; a list holds 16 to 64 rows; in every draw one owner index receives 64 rows from every device, and one device fills all its lists. `hist_slot`: every entry names a filled slot of the request lists of the device that holds the user.
All inputs are finite; a program needn't handle non-finite values.
Results may differ from the reference program's by a relative error of at most 0.025.
Values may be sent and summed in bfloat16 or wider, within the bound.
No kernel may reach another device: no remote copies, remote signals or barrier semaphores. Data moves between devices by JAX's collectives and lax.ppermute only.
A program may use at most 128 MiB of HBM per device.

```python
import math
from functools import partial
import jax
import jax.numpy as jnp
from jax import lax

D = 768
HID = 3072
F = 8
L = 50
CAP = 64
V_DEV = 128
U_DEV = 16
USERS = 2048
N_DP = 16
DEVICES = 128


def request_plan(key):
    plan_keys = jax.random.split(jax.random.fold_in(key, 211), 3)
    hot_owner = jax.random.randint(plan_keys[0], (), 0, N_DP)
    full_device = jax.random.randint(plan_keys[1], (), 0, DEVICES)
    counts = jax.random.randint(plan_keys[2], (DEVICES, N_DP), CAP // 4, CAP + 1)
    owner_ids = jnp.arange(N_DP, dtype=jnp.int32).reshape(1, N_DP)
    device_ids = jnp.arange(DEVICES, dtype=jnp.int32).reshape(DEVICES, 1)
    counts = jnp.where((owner_ids == hot_owner) | (device_ids == full_device), CAP, counts)
    return (counts, full_device)


def draw_pool_query(key, part):
    key = jax.random.fold_in(key, 1)
    return jnp.clip(jax.random.normal(key, (D,), jnp.float32), -4.0, 4.0)


def draw_frames(key, part):
    key = jax.random.fold_in(key, 2)
    sub_keys = jax.random.split(key, 1)
    video_total = V_DEV * N_DP
    return jnp.clip(jax.random.normal(sub_keys[0], (video_total, F, D), jnp.float32), -4.0, 4.0).astype(jnp.bfloat16)


def draw_w_qkv(key, part):
    key = jax.random.fold_in(key, 3)
    sub_keys = jax.random.split(key, 1)
    return (jnp.clip(jax.random.normal(sub_keys[0], (D, 3 * D), jnp.float32), -5.0, 5.0) / D ** 0.5).astype(jnp.bfloat16)


def draw_request_rows(key, part):
    counts, full_device = request_plan(key)
    key = jax.random.fold_in(key, 4)
    ranked = jax.random.randint(key, (DEVICES, N_DP, V_DEV), 0, 1 << 20) * V_DEV + jnp.arange(V_DEV, dtype=jnp.int32)
    order = jnp.argsort(ranked, axis=-1)[..., :CAP].astype(jnp.int32)
    slot_ids = jnp.arange(CAP, dtype=jnp.int32).reshape(1, 1, CAP)
    return jnp.where(slot_ids < counts[..., None], order, -1)


def draw_hist_slot(key, part):
    counts, full_device = request_plan(key)
    key = jax.random.fold_in(key, 5)
    sub_keys = jax.random.split(key, 3)
    positions = U_DEV * L
    owner_pick = jax.random.randint(sub_keys[0], (DEVICES, positions), 0, N_DP)
    raw_pick = jax.random.randint(sub_keys[1], (DEVICES, positions), 0, 1 << 20)
    filled = jnp.take_along_axis(counts, owner_pick, axis=1)
    slots = owner_pick * CAP + raw_pick % filled
    chosen_position = jax.random.randint(sub_keys[2], (), 0, positions)
    device_ids = jnp.arange(DEVICES, dtype=jnp.int32).reshape(DEVICES, 1)
    position_ids = jnp.arange(positions, dtype=jnp.int32).reshape(1, positions)
    slots = jnp.where((device_ids == full_device) & (position_ids == chosen_position), N_DP * CAP - 1, slots)
    return slots.reshape(USERS, L).astype(jnp.int32)


def draw_hist_len(key, part):
    key = jax.random.fold_in(key, 6)
    sub_keys = jax.random.split(key, 2)
    lengths = jax.random.randint(sub_keys[0], (USERS,), 1, L + 1)
    longest = jax.random.randint(sub_keys[1], (), 0, USERS)
    return jnp.where(jnp.arange(USERS, dtype=jnp.int32) == longest, L, lengths).astype(jnp.int32)


def block_levels(stream_key, shape, pieces, low, high):
    gain, own = 1.0, jax.random.fold_in(stream_key, 6)
    for axis_at, parts in pieces:
        heights = jnp.exp(jax.random.uniform(jax.random.fold_in(own, axis_at), (parts,), jnp.float32, low / len(pieces), high / len(pieces)))
        gain = gain * jnp.repeat(heights, shape[axis_at] // parts).reshape([-1 if axis == axis_at else 1 for axis in range(len(shape))])
    return gain


def bell_draw(rng, extent, width, most, shards=(), kind=jnp.bfloat16):
    values = jax.random.normal(rng, extent, jnp.float32) * width
    if len(shards) > 0:
        values = block_levels(rng, extent, shards, -0.22, 0.18) * values
    return jnp.clip(values, min=-most, max=most).astype(kind)


def setup_inputs(seed: int = 0) -> dict:
    splits = jax.random.split(jax.random.key(seed), 14)
    return {
        "frames": draw_frames(jax.random.fold_in(splits[13], 71), 0),
        "frame_gain": jnp.clip(1.0 + 0.15 * jax.random.normal(splits[1], (D,), jnp.float32), 0.25, 1.75),
        "w_up": bell_draw(splits[2], (D, HID), D ** -0.5, 0.21875),
        "w_down": bell_draw(splits[3], (HID, D), HID ** -0.5, 0.109375),
        "pool_query": draw_pool_query(jax.random.fold_in(splits[13], 71), 0),
        "pos_embed": bell_draw(splits[5], (L, D), 1.0, 5.0),
        "user_gain": jnp.clip(1.0 + 0.15 * jax.random.normal(splits[6], (D,), jnp.float32), 0.25, 1.75),
        "w_qkv": draw_w_qkv(jax.random.fold_in(splits[13], 71), 0),
        "w_out": bell_draw(splits[8], (D, D), D ** -0.5, 0.21875),
        "request_rows": draw_request_rows(jax.random.fold_in(splits[13], 71), 0),
        "hist_slot": draw_hist_slot(jax.random.fold_in(splits[13], 71), 0),
        "hist_len": draw_hist_len(jax.random.fold_in(splits[13], 71), 0),
        "d_encoded": bell_draw(splits[12], (USERS, L, D), 1.0, 6.0, ((0, 128),)),
    }


epsilon = 1e-06
masked_score = -1000000000.0

def layer_norm(values, norm_gain):
    row_mean = lax.optimization_barrier(jnp.mean(values, axis=-1, keepdims=True))
    centred = values - row_mean
    variance = lax.optimization_barrier(jnp.mean(centred * centred, axis=-1, keepdims=True))
    return centred * lax.rsqrt(variance + epsilon) * norm_gain

def frame_block(frames32, norm_gain, w_up, w_down):
    normed = layer_norm(frames32, norm_gain).astype(jnp.bfloat16)
    hidden = jax.nn.gelu(jnp.dot(normed, w_up, preferred_element_type=jnp.float32)).astype(jnp.bfloat16)
    return frames32 + jnp.dot(hidden, w_down, preferred_element_type=jnp.float32)

def user_encoder(inputs, norm_gain, w_qkv, w_out, lengths):
    user_count, seq_length, feature_width = inputs.shape
    normed = layer_norm(inputs, norm_gain).astype(jnp.bfloat16).reshape(user_count * seq_length, feature_width)
    packed = jnp.dot(normed, w_qkv, preferred_element_type=jnp.float32).astype(jnp.bfloat16)
    packed = packed.reshape(user_count, seq_length, 3 * feature_width)
    query_part = packed[..., :feature_width].astype(jnp.float32)
    key_part = packed[..., feature_width:2 * feature_width].astype(jnp.float32)
    value_part = packed[..., 2 * feature_width:].astype(jnp.float32)
    attn_scores = jnp.einsum('usd,utd->ust', query_part, key_part) / math.sqrt(feature_width)
    positions = jnp.arange(seq_length, dtype=jnp.int32)
    allowed = (positions[None, None, :] <= positions[None, :, None]) & (positions[None, None, :] < lengths[:, None, None])
    attn_scores = jnp.where(allowed, attn_scores, masked_score)
    attn_probs = jax.nn.softmax(attn_scores, axis=-1).astype(jnp.bfloat16)
    attended = jnp.einsum('ust,utd->usd', attn_probs.astype(jnp.float32), value_part).astype(jnp.bfloat16)
    projected = jnp.dot(attended.reshape(user_count * seq_length, feature_width), w_out, preferred_element_type=jnp.float32)
    updated = inputs + projected.reshape(inputs.shape)
    live_rows = positions[None, :] < lengths[:, None]
    return jnp.where(live_rows[..., None], updated, 0.0)

def reference(frames, frame_gain, w_up, w_down, pool_query, pos_embed, user_gain, w_qkv, w_out, request_rows, hist_slot, hist_len, d_encoded):
    video_total = V_DEV * N_DP
    flat_frames = frames.reshape(video_total * F, D).astype(jnp.float32)
    raw_out, frame_back = jax.vjp(partial(frame_block, norm_gain=frame_gain, w_up=w_up, w_down=w_down), flat_frames)
    framed = raw_out.astype(jnp.bfloat16).reshape(video_total, F, D).astype(jnp.float32)
    pool_scores = lax.optimization_barrier(jnp.sum(framed * pool_query, axis=-1)) / math.sqrt(D)
    pool_weights = jax.nn.softmax(pool_scores, axis=-1)
    pooled = lax.optimization_barrier(jnp.sum(pool_weights[..., None] * framed, axis=1))
    pooled_table = pooled.astype(jnp.bfloat16)
    device_row = (jnp.arange(USERS, dtype=jnp.int32) // U_DEV)[:, None]
    owner_index = hist_slot // CAP
    column = hist_slot % CAP
    video_of = (owner_index * V_DEV + request_rows[device_row, owner_index, column]).astype(jnp.int32)
    inputs = pooled_table[video_of].astype(jnp.float32) + pos_embed.astype(jnp.float32)[None]
    encoded32, encoder_back = jax.vjp(partial(user_encoder, norm_gain=user_gain, w_qkv=w_qkv, w_out=w_out, lengths=hist_len), inputs)
    d_inputs, = encoder_back(d_encoded.astype(jnp.float32))
    d_pooled = jax.ops.segment_sum(d_inputs.reshape(-1, D), video_of.reshape(-1), num_segments=video_total)
    cross_dots = lax.optimization_barrier(jnp.sum(d_pooled[:, None, :] * framed, axis=-1))
    self_dot = lax.optimization_barrier(jnp.sum(d_pooled * pooled, axis=-1))
    d_frame_out = pool_weights[..., None] * (d_pooled[:, None, :] + ((cross_dots - self_dot[:, None]) / math.sqrt(D))[..., None] * pool_query)
    d_flat, = frame_back(d_frame_out.reshape(video_total * F, D))
    return (encoded32.astype(jnp.bfloat16), d_flat.astype(jnp.bfloat16).reshape(video_total, F, D))
```

```python
import functools
import math

import jax
import jax.numpy as jnp
from jax import lax
from jax.experimental import pallas as pl
from jax.experimental.pallas import tpu as pltpu
from jax.sharding import PartitionSpec as P

D = 768
HID = 3072
L = 50
LP = 56
USERS = 16
GROUP = 4
ROWS = GROUP * LP
OWNERS = 16
HALF = 64
CAP = 64
PAY = D + 128
EPS = 1e-6
ROOT = math.sqrt(D)
MASKED = -1e9
AXES = ("dp", "frame")
f32 = jnp.float32
bf16 = jnp.bfloat16
VMEM = pl.BlockSpec(memory_space=pltpu.VMEM)
SMEM = pl.BlockSpec(memory_space=pltpu.SMEM)


def dot_nn(a, b):
    return lax.dot_general(a, b, (((1,), (0,)), ((), ())), preferred_element_type=f32)


def dot_nt(a, b):
    return lax.dot_general(a, b, (((1,), (1,)), ((), ())), preferred_element_type=f32)


def dot_tn(a, b):
    return lax.dot_general(a, b, (((0,), (0,)), ((), ())), preferred_element_type=f32)


def params(megabytes):
    return pltpu.CompilerParams(vmem_limit_bytes=megabytes << 20)


def normalised(x):
    centred = x - jnp.mean(x, axis=-1, keepdims=True)
    rstd = lax.rsqrt(jnp.mean(centred * centred, axis=-1, keepdims=True) + EPS)
    return centred * rstd, rstd


def norm_back(d_normed, gain, xhat, rstd):
    d_hat = d_normed * gain
    along = jnp.mean(d_hat * xhat, axis=-1, keepdims=True)
    return rstd * (d_hat - jnp.mean(d_hat, axis=-1, keepdims=True) - xhat * along)


def frame_forward(core, frames, gain, w_up, w_down, mine, other, out, slope, normed, total):
    step = pl.program_id(0)

    @pl.when(step == 0)
    def _():
        x = frames[...].astype(f32)
        xhat, _ = normalised(x)
        normed[...] = (xhat * gain[...]).astype(bf16)
        total[...] = x

    a = dot_nn(normed[...], w_up[...])
    c0 = math.sqrt(2.0 / math.pi)
    square = a * a
    th = jnp.tanh(c0 * a * (1.0 + 0.044715 * square))
    half = 0.5 * (1.0 + th)
    hidden = (a * half).astype(bf16)
    slope[...] = (half + 0.5 * a * (1.0 - th * th) * c0 * (1.0 + 3 * 0.044715 * square)).astype(bf16)
    total[...] += dot_nn(hidden, w_down[...])

    @pl.when(step == pl.num_programs(0) - 1)
    def _():
        out[...] = total[...].astype(bf16)
        c = core[0]
        mine[...] = total[pl.ds(pl.multiple_of(c * HALF, HALF), HALF), :].astype(bf16)
        other[...] = total[pl.ds(pl.multiple_of((1 - c) * HALF, HALF), HALF), :].astype(bf16)


def run_frame_forward(core, frames, gain, w_up, w_down):
    steps = 4
    width = HID // steps
    rows = frames.shape[0]
    full = lambda r, w: pl.BlockSpec((r, w), lambda j: (0, 0))
    return pl.pallas_call(
        frame_forward,
        grid=(steps,),
        in_specs=[
            SMEM,
            full(rows, D),
            full(1, D),
            pl.BlockSpec((D, width), lambda j: (0, j)),
            pl.BlockSpec((width, D), lambda j: (j, 0)),
        ],
        out_specs=[full(HALF, D), full(HALF, D), full(rows, D), pl.BlockSpec((rows, width), lambda j: (0, j))],
        out_shape=[
            jax.ShapeDtypeStruct((HALF, D), bf16),
            jax.ShapeDtypeStruct((HALF, D), bf16),
            jax.ShapeDtypeStruct((rows, D), bf16),
            jax.ShapeDtypeStruct((rows, HID), bf16),
        ],
        scratch_shapes=[pltpu.VMEM((rows, D), bf16), pltpu.VMEM((rows, D), f32)],
        compiler_params=params(40),
        name="frame_forward",
    )(core, frames, gain, w_up, w_down)


def pieces(value):
    first = value.astype(bf16).astype(f32)
    rest = value - first
    second = rest.astype(bf16).astype(f32)
    return first, second, rest - second


def write_payload(out, mean, top, total):
    lane = lax.broadcasted_iota(jnp.int32, (HALF, 128), 1)
    stats = jnp.zeros((HALF, 128), f32)
    for at, piece in enumerate(pieces(top) + pieces(total)):
        stats = jnp.where(lane == at, piece, stats)
    out[:, :D] = mean.astype(bf16)
    out[:, D:] = stats.astype(bf16)


def read_stats(block):
    stats = block[:, D:].astype(f32)
    lane = lax.broadcasted_iota(jnp.int32, stats.shape, 1)
    top = jnp.sum(jnp.where(lane < 3, stats, 0.0), axis=-1, keepdims=True)
    total = jnp.sum(jnp.where((lane >= 3) & (lane < 6), stats, 0.0), axis=-1, keepdims=True)
    return top, total


def pool_pair(mine, theirs, query, out):
    a = mine[...].astype(f32)
    b = theirs[...].astype(f32)
    q = query[...]
    score_a = jnp.sum(a * q, axis=-1, keepdims=True) / ROOT
    score_b = jnp.sum(b * q, axis=-1, keepdims=True) / ROOT
    top = jnp.maximum(score_a, score_b)
    weight_a = jnp.exp(score_a - top)
    weight_b = jnp.exp(score_b - top)
    total = weight_a + weight_b
    write_payload(out, (weight_a * a + weight_b * b) / total, top, total)


def pool_all(p0, p1, p2, p3, spread, out):
    parts = (p0, p1, p2, p3)
    stats = [read_stats(p) for p in parts]
    top = functools.reduce(jnp.maximum, [s[0] for s in stats])
    weights = [jnp.exp(s[0] - top) * s[1] for s in stats]
    total = sum(weights)
    mean = sum(w * p[:, :D].astype(f32) for w, p in zip(weights, parts)) / total
    write_payload(out, mean, top, total)
    rows = mean.astype(bf16)
    for o in range(OWNERS):
        spread[o] = rows


def encoder(
    lens, own_index, other_index, own_table, other_table, pos, gain, w_qkv, w_out, d_encoded,
    encoded, d_inputs, d_wide, e_wide,
):
    step = pl.program_id(0)

    @pl.when(step == 0)
    def _():
        for j in range(D // 128):
            d_wide[j] = d_encoded[:, j * 128 : (j + 1) * 128].astype(f32)

    at = lax.broadcasted_iota(jnp.int32, (ROWS, OWNERS * HALF), 1)
    x = dot_nn((at == own_index[...]).astype(bf16), own_table[...])
    x = x + dot_nn((at == other_index[...]).astype(bf16), other_table[...])
    x = x + pos[...]
    xhat, rstd = normalised(x)
    g = gain[...]
    packed = dot_nn((xhat * g).astype(bf16), w_qkv[...]).astype(bf16)
    q, k, v = packed[:, :D], packed[:, D : 2 * D], packed[:, 2 * D :]

    place = lax.broadcasted_iota(jnp.int32, (ROWS, 1), 0)
    length = jnp.full((ROWS, 1), 0, jnp.int32)
    first = jnp.full((ROWS, 1), 0, jnp.int32)
    for u in range(GROUP):
        here = (place >= u * LP) & (place < (u + 1) * LP)
        length = jnp.where(here, lens[step * GROUP + u], length)
        first = jnp.where(here, u * LP, first)
    column = lax.broadcasted_iota(jnp.int32, (ROWS, ROWS), 1)
    allowed = (column >= first) & (column <= place) & (column < first + length)
    live = (place - first) < length

    scores = jnp.where(allowed, dot_nt(q, k) / ROOT, MASKED)
    raised = jnp.exp(scores - jnp.max(scores, axis=-1, keepdims=True))
    probs = raised / jnp.sum(raised, axis=-1, keepdims=True)
    probs16 = probs.astype(bf16)
    attended = dot_nn(probs16, v).astype(bf16)
    updated = jnp.where(live, x + dot_nn(attended, w_out[...]), 0.0)
    cotangent = []
    for u in range(GROUP):
        rows = pl.ds(step * GROUP + u, L, stride=USERS)
        for j in range(D // 128):
            e_wide[j, rows, :] = updated[u * LP : u * LP + L, j * 128 : (j + 1) * 128]

    for u in range(GROUP):
        rows = pl.ds(step * GROUP + u, L, stride=USERS)
        one = jnp.concatenate([d_wide[j, rows, :] for j in range(D // 128)], axis=1)
        cotangent.append(jnp.concatenate([one, jnp.zeros((LP - L, D), f32)], axis=0))
    d_out = jnp.where(live, jnp.concatenate(cotangent, axis=0), 0.0)
    d_attended = dot_nt(d_out.astype(bf16), w_out[...]).astype(bf16)
    d_probs = dot_nt(d_attended, v).astype(bf16).astype(f32)
    d_v = dot_tn(probs16, d_attended).astype(bf16)
    d_scores = probs * (d_probs - jnp.sum(d_probs * probs, axis=-1, keepdims=True)) / ROOT
    d_scores = d_scores.astype(bf16)
    d_q = dot_nn(d_scores, k).astype(bf16)
    d_k = dot_tn(d_scores, q).astype(bf16)
    d_normed = dot_nt(d_q, w_qkv[:, :D]) + dot_nt(d_k, w_qkv[:, D : 2 * D]) + dot_nt(d_v, w_qkv[:, 2 * D :])
    d_normed = d_normed.astype(bf16).astype(f32)
    d_inputs[...] = (d_out + norm_back(d_normed, g, xhat, rstd)).astype(bf16)

    @pl.when(step == pl.num_programs(0) - 1)
    def _():
        for j in range(D // 128):
            encoded[:, j * 128 : (j + 1) * 128] = e_wide[j].astype(bf16)


def run_encoder(lens, own_index, other_index, own_table, other_table, pos, gain, w_qkv, w_out, d_encoded):
    full = lambda r, w: pl.BlockSpec((r, w), lambda j: (0, 0))
    part = lambda w: pl.BlockSpec((ROWS, w), lambda j: (j, 0))
    count = USERS * L
    return pl.pallas_call(
        encoder,
        grid=(USERS // GROUP,),
        in_specs=[
            SMEM, part(1), part(1), full(OWNERS * HALF, D), full(OWNERS * HALF, D), full(ROWS, D), full(1, D),
            full(D, 3 * D), full(D, D), full(count, D),
        ],
        out_specs=[full(count, D), part(D)],
        out_shape=[
            jax.ShapeDtypeStruct((count, D), bf16),
            jax.ShapeDtypeStruct((USERS * LP, D), bf16),
        ],
        scratch_shapes=[pltpu.VMEM((D // 128, count, 128), f32)] * 2,
        compiler_params=params(56),
        name="user_encoder",
    )(lens, own_index, other_index, own_table, other_table, pos, gain, w_qkv, w_out, d_encoded)


def scatter(own_index, peer_index, own_rows, peer_rows, out):
    count = USERS * LP
    block = out.shape[0]
    row = lax.broadcasted_iota(jnp.int32, (block, count), 0) + pl.program_id(0) * block
    total = dot_nn((row == own_index[...]).astype(bf16), own_rows[...])
    total = total + dot_nn((row == peer_index[...]).astype(bf16), peer_rows[...])
    out[...] = total.astype(bf16)


def run_scatter(own_index, peer_index, own_rows, peer_rows):
    count = USERS * LP
    steps = 4
    full = lambda r, w: pl.BlockSpec((r, w), lambda j: (0, 0))
    return pl.pallas_call(
        scatter,
        grid=(steps,),
        in_specs=[full(1, count), full(1, count), full(count, D), full(count, D)],
        out_specs=pl.BlockSpec((OWNERS * HALF // steps, D), lambda j: (j, 0)),
        out_shape=jax.ShapeDtypeStruct((OWNERS * HALF, D), bf16),
        compiler_params=params(40),
        name="scatter",
    )(own_index, peer_index, own_rows, peer_rows)


def frame_backward(
    core, d_mine, d_other, pay_mine, pay_other, query, frames, framed, gain, slope, w_up, w_down,
    out, grad, grad16, total, d_pooled, pay,
):
    step = pl.program_id(0)

    @pl.when(step == 0)
    def _():
        c = core[0]
        here = pl.ds(pl.multiple_of(c * HALF, HALF), HALF)
        there = pl.ds(pl.multiple_of((1 - c) * HALF, HALF), HALF)
        d_pooled[here, :] = d_mine[...].astype(f32)
        d_pooled[there, :] = d_other[...].astype(f32)
        pay[here, :] = pay_mine[...].astype(f32)
        pay[there, :] = pay_other[...].astype(f32)
        x = framed[...].astype(f32)
        q = query[...]
        top, whole = read_stats(pay)
        weight = jnp.exp(jnp.sum(x * q, axis=-1, keepdims=True) / ROOT - top) / whole
        dp = d_pooled[...]
        cross = jnp.sum(dp * x, axis=-1, keepdims=True)
        own = jnp.sum(dp * pay[:, :D], axis=-1, keepdims=True)
        d_out = weight * (dp + ((cross - own) / ROOT) * q)
        grad[...] = d_out
        grad16[...] = d_out.astype(bf16)
        total[...] = jnp.zeros_like(total)

    d_hidden = dot_nt(grad16[...], w_down[...]).astype(bf16).astype(f32)
    d_a = (d_hidden * slope[...].astype(f32)).astype(bf16)
    total[...] += dot_nt(d_a, w_up[...])

    @pl.when(step == pl.num_programs(0) - 1)
    def _():
        xhat, rstd = normalised(frames[...].astype(f32))
        d_normed = total[...].astype(bf16).astype(f32)
        out[...] = (grad[...] + norm_back(d_normed, gain[...], xhat, rstd)).astype(bf16)


def run_frame_backward(core, d_mine, d_other, pay_mine, pay_other, query, frames, framed, gain, slope, w_up, w_down):
    steps = 4
    width = HID // steps
    rows = frames.shape[0]
    full = lambda r, w: pl.BlockSpec((r, w), lambda j: (0, 0))
    return pl.pallas_call(
        frame_backward,
        grid=(steps,),
        in_specs=[
            SMEM, full(HALF, D), full(HALF, D), full(HALF, PAY), full(HALF, PAY), full(1, D), full(rows, D),
            full(rows, D), full(1, D),
            pl.BlockSpec((rows, width), lambda j: (0, j)),
            pl.BlockSpec((D, width), lambda j: (0, j)),
            pl.BlockSpec((width, D), lambda j: (j, 0)),
        ],
        out_specs=full(rows, D),
        out_shape=jax.ShapeDtypeStruct((rows, D), bf16),
        scratch_shapes=[
            pltpu.VMEM((rows, D), f32), pltpu.VMEM((rows, D), bf16), pltpu.VMEM((rows, D), f32),
            pltpu.VMEM((rows, D), f32), pltpu.VMEM((rows, PAY), f32),
        ],
        compiler_params=params(40),
        name="frame_backward",
    )(core, d_mine, d_other, pay_mine, pay_other, query, frames, framed, gain, slope, w_up, w_down)


def swap_with(x, bits):
    pairs = [(i, i ^ bits) for i in range(8)]
    return lax.ppermute(x, "frame", pairs)


def spread_along_x(x):
    return [swap_with(x, 2 * k) for k in (1, 2, 3)]


def shards(
    frames, frame_gain, w_up, w_down, pool_query, pos_embed, user_gain, w_qkv, w_out,
    request_rows, hist_slot, hist_len, d_encoded,
):
    rows = frames.shape[0]
    c = lax.axis_index("frame") % 2
    core = c.astype(jnp.int32).reshape(1)
    flat_frames = frames.reshape(rows, D)
    gain = frame_gain.reshape(1, D)
    query = pool_query.reshape(1, D)

    mine, other, framed, slope = run_frame_forward(core, flat_frames, gain, w_up, w_down)
    theirs = swap_with(other, 1)
    payload = jax.ShapeDtypeStruct((HALF, PAY), bf16)
    pair = pl.pallas_call(
        pool_pair, in_specs=[VMEM] * 3, out_specs=VMEM, out_shape=payload, name="pool_pair",
    )(mine, theirs, query)
    spread, pay_mine = pl.pallas_call(
        pool_all, in_specs=[VMEM] * 4, out_specs=[VMEM] * 2,
        out_shape=[jax.ShapeDtypeStruct((OWNERS, HALF, D), bf16), payload], name="pool_all",
    )(pair, *spread_along_x(pair))
    table = lax.all_to_all(spread, "dp", split_axis=0, concat_axis=0, tiled=True).reshape(OWNERS * HALF, D)
    other_table = swap_with(table, 1)
    pay_other = swap_with(pay_mine, 1)

    slots = jnp.pad(hist_slot, ((0, 0), (0, LP - L)), constant_values=-1).reshape(USERS * LP, 1)
    known = jnp.arange(OWNERS * CAP, dtype=jnp.int32)[None, :]
    local = jnp.sum(jnp.where(slots == known, request_rows.reshape(1, OWNERS * CAP), 0), axis=1, keepdims=True)
    position = jnp.where(slots >= 0, (slots // CAP) * HALF + local % HALF, -1)
    own_index = jnp.where(local // HALF == c, position, -1)
    other_index = jnp.where(local // HALF == c, -1, position)
    peer_index = swap_with(other_index.reshape(1, USERS * LP), 1)

    pos = jnp.tile(jnp.pad(pos_embed.astype(f32), ((0, LP - L), (0, 0))), (GROUP, 1))
    cotangent = jnp.transpose(d_encoded, (1, 0, 2)).reshape(USERS * L, D)
    encoded, d_inputs = run_encoder(
        hist_len, own_index, other_index, table, other_table, pos, user_gain.reshape(1, D), w_qkv, w_out, cotangent
    )
    peer_rows = swap_with(d_inputs, 1)
    d_table = run_scatter(own_index.reshape(1, USERS * LP), peer_index, d_inputs, peer_rows)
    returned = lax.all_to_all(
        d_table.reshape(OWNERS, HALF, D), "dp", split_axis=0, concat_axis=0, tiled=True
    )
    partial = jnp.sum(returned.astype(f32), axis=0).astype(bf16)
    d_mine = sum(part.astype(f32) for part in [partial] + spread_along_x(partial)).astype(bf16)
    d_other = swap_with(d_mine, 1)
    d_frames = run_frame_backward(
        core, d_mine, d_other, pay_mine, pay_other, query, flat_frames, framed, gain, slope, w_up, w_down
    )
    encoded = jnp.transpose(encoded.reshape(L, USERS, D), (1, 0, 2))
    return encoded, d_frames.reshape(rows, 1, D)


def solution(mesh):
    in_specs = (
        P("dp", "frame", None),
        P(),
        P(),
        P(),
        P(),
        P(),
        P(),
        P(),
        P(),
        P(("dp", "frame"), None, None),
        P(("dp", "frame"), None),
        P(("dp", "frame")),
        P(("dp", "frame"), None, None),
    )
    out_specs = (P(("dp", "frame"), None, None), P("dp", "frame", None))
    return jax.shard_map(shards, mesh=mesh, in_specs=in_specs, out_specs=out_specs, check_vma=False)
```

```python
import functools
import math

import jax
import jax.numpy as jnp
from jax import lax
from jax.experimental import pallas as pl
from jax.experimental.pallas import tpu as pltpu
from jax.sharding import PartitionSpec as P

D = 768
HID = 3072
L = 50
LP = 56
USERS = 16
GROUP = 8
ROWS = GROUP * LP
SUB = 4
SUB_ROWS = SUB * LP
ENC_MB = 28
OWNERS = 16
HALF = 64
CAP = 64
PAY = D + 128
EPS = 1e-6
ROOT = math.sqrt(D)
MASKED = -1e9
AXES = ("dp", "frame")
f32 = jnp.float32
bf16 = jnp.bfloat16
VMEM = pl.BlockSpec(memory_space=pltpu.VMEM)
SMEM = pl.BlockSpec(memory_space=pltpu.SMEM)
ANY = pl.BlockSpec(memory_space=pl.ANY)
HBM = pl.BlockSpec(memory_space=pltpu.HBM)
PARTS = 4
FRAME_MB = 16


def dot_nn(a, b):
    return lax.dot_general(a, b, (((1,), (0,)), ((), ())), preferred_element_type=f32)


def dot_nt(a, b):
    return lax.dot_general(a, b, (((1,), (1,)), ((), ())), preferred_element_type=f32)


def dot_tn(a, b):
    return lax.dot_general(a, b, (((0,), (0,)), ((), ())), preferred_element_type=f32)


def in_vmem(x):
    return pltpu.with_memory_space_constraint(x, pltpu.VMEM)


def in_hbm(x):
    return pltpu.with_memory_space_constraint(x, pltpu.HBM)


def params(megabytes):
    return pltpu.CompilerParams(vmem_limit_bytes=megabytes << 20)


def cost(flops, moved):
    return pl.CostEstimate(flops=int(flops), bytes_accessed=int(moved), transcendentals=0)


def normalised(x):
    centred = x - jnp.mean(x, axis=-1, keepdims=True)
    rstd = lax.rsqrt(jnp.mean(centred * centred, axis=-1, keepdims=True) + EPS)
    return centred * rstd, rstd


def norm_back(d_normed, gain, xhat, rstd):
    d_hat = d_normed * gain
    along = jnp.mean(d_hat * xhat, axis=-1, keepdims=True)
    return rstd * (d_hat - jnp.mean(d_hat, axis=-1, keepdims=True) - xhat * along)


def fetch(source, target, sems, axis, parts):
    width = source.shape[axis] // parts
    copies = []
    for p in range(parts):
        cut = pl.ds(p * width, width)
        where = (cut, slice(None)) if axis == 0 else (slice(None), cut)
        copies.append(pltpu.make_async_copy(source.at[where], target.at[where], sems.at[p]))
    return copies


def frame_forward(
    core, frames_in, gain_in, w_up, w_down, mine, other, out, slope, up, down, frames, gain, sems, up_sems, down_sems
):
    first = [pltpu.make_async_copy(frames_in, frames, sems.at[0]), pltpu.make_async_copy(gain_in, gain, sems.at[1])]
    for one in first:
        one.start()
    ups = fetch(w_up, up, up_sems, 1, PARTS)
    downs = fetch(w_down, down, down_sems, 0, PARTS)
    for one, two in zip(ups, downs):
        one.start()
        two.start()
    for one in first:
        one.wait()
    x = frames[...].astype(f32)
    xhat, _ = normalised(x)
    normed = (xhat * gain[...][None, :]).astype(bf16)
    total = x
    width = HID // PARTS
    c0 = math.sqrt(2.0 / math.pi)
    for p in range(PARTS):
        cut = pl.ds(p * width, width)
        ups[p].wait()
        a = dot_nn(normed, up[:, cut])
        square = a * a
        th = jnp.tanh(c0 * a * (1.0 + 0.044715 * square))
        half = 0.5 * (1.0 + th)
        hidden = (a * half).astype(bf16)
        slope[:, cut] = (half + 0.5 * a * (1.0 - th * th) * c0 * (1.0 + 3 * 0.044715 * square)).astype(bf16)
        downs[p].wait()
        total = total + dot_nn(hidden, down[cut, :])
    stored = total.astype(bf16)
    out[...] = stored
    upper = core[0] == 1
    mine[...] = jnp.where(upper, stored[HALF:], stored[:HALF])
    other[...] = jnp.where(upper, stored[:HALF], stored[HALF:])


def run_frame_forward(core, frames, gain, w_up, w_down):
    rows = frames.shape[0]
    return pl.pallas_call(
        frame_forward,
        in_specs=[SMEM, HBM, HBM, HBM, HBM],
        out_specs=[VMEM] * 6,
        out_shape=[
            jax.ShapeDtypeStruct((HALF, D), bf16),
            jax.ShapeDtypeStruct((HALF, D), bf16),
            jax.ShapeDtypeStruct((rows, D), bf16),
            jax.ShapeDtypeStruct((rows, HID), bf16),
            pltpu.VMEM((D, HID), bf16),
            pltpu.VMEM((HID, D), bf16),
        ],
        scratch_shapes=[
            pltpu.VMEM((rows, D), bf16), pltpu.VMEM((D,), f32), pltpu.SemaphoreType.DMA((2,)),
            pltpu.SemaphoreType.DMA((PARTS,)), pltpu.SemaphoreType.DMA((PARTS,)),
        ],
        compiler_params=params(FRAME_MB),
        name="frame_forward",
    )(core, in_hbm(frames), in_hbm(gain), in_hbm(w_up), in_hbm(w_down))


def pieces(value):
    first = value.astype(bf16).astype(f32)
    rest = value - first
    second = rest.astype(bf16).astype(f32)
    return first, second, rest - second


def write_payload(out, mean, top, total):
    lane = lax.broadcasted_iota(jnp.int32, (HALF, 128), 1)
    stats = jnp.zeros((HALF, 128), f32)
    for at, piece in enumerate(pieces(top) + pieces(total)):
        stats = jnp.where(lane == at, piece, stats)
    out[:, :D] = mean.astype(bf16)
    out[:, D:] = stats.astype(bf16)


def read_stats(block):
    stats = block[:, D:].astype(f32)
    lane = lax.broadcasted_iota(jnp.int32, stats.shape, 1)
    top = jnp.sum(jnp.where(lane < 3, stats, 0.0), axis=-1, keepdims=True)
    total = jnp.sum(jnp.where((lane >= 3) & (lane < 6), stats, 0.0), axis=-1, keepdims=True)
    return top, total


def pool_pair(mine, theirs, query, out):
    a = mine[...].astype(f32)
    b = theirs[...].astype(f32)
    q = query[...][None, :]
    score_a = jnp.sum(a * q, axis=-1, keepdims=True) / ROOT
    score_b = jnp.sum(b * q, axis=-1, keepdims=True) / ROOT
    top = jnp.maximum(score_a, score_b)
    weight_a = jnp.exp(score_a - top)
    weight_b = jnp.exp(score_b - top)
    total = weight_a + weight_b
    write_payload(out, (weight_a * a + weight_b * b) / total, top, total)


def pool_all(p0, p1, p2, p3, *rest):
    spread, out = rest[-2:]
    parts = (p0, p1, p2, p3)
    stats = [read_stats(p) for p in parts]
    top = functools.reduce(jnp.maximum, [s[0] for s in stats])
    weights = [jnp.exp(s[0] - top) * s[1] for s in stats]
    total = sum(weights)
    mean = sum(w * p[:, :D].astype(f32) for w, p in zip(weights, parts)) / total
    write_payload(out, mean, top, total)
    rows = mean.astype(bf16)
    for o in range(OWNERS):
        spread[o] = rows


def prepare(
    core, lens, slots, requests, d_encoded, w_out, w_qkv, after,
    d_out, d_attended, own_column, other_column, own_row, other_row, qkv, d_wide, sem,
):
    load = pltpu.make_async_copy(w_qkv, qkv, sem)
    load.start()
    c = core[0]
    lane = lax.broadcasted_iota(jnp.int32, (LP, L), 1)
    diagonal = lane == lax.broadcasted_iota(jnp.int32, (LP, L), 0)
    inside = lax.broadcasted_iota(jnp.int32, (LP, 1), 0) < L
    owner_lane = lax.broadcasted_iota(jnp.int32, (LP, OWNERS), 1)
    cap_lane = lax.broadcasted_iota(jnp.int32, (LP, CAP), 1)
    asked = requests[0].astype(f32).astype(bf16)
    for u in range(USERS):
        slot = jnp.sum(jnp.where(diagonal, slots[u : u + 1, :].astype(f32), 0.0), axis=1, keepdims=True)
        slot = slot.astype(jnp.int32)
        owner = slot >> 6
        lists = dot_nn((owner_lane == owner).astype(bf16), asked)
        local = jnp.sum(jnp.where(cap_lane == (slot & (CAP - 1)), lists, 0.0), axis=1, keepdims=True)
        local = local.astype(jnp.int32)
        position = jnp.where(inside, owner * HALF + (local & (HALF - 1)), -1)
        own = (local >> 6) == c
        here = pl.ds(u * LP, LP)
        own_column[here, :] = jnp.where(own, position, -1)
        other_column[here, :] = jnp.where(own, -1, position)
    square = (128, 128)
    same = lax.broadcasted_iota(jnp.int32, square, 0) == lax.broadcasted_iota(jnp.int32, square, 1)
    for part in range(USERS * LP // 128):
        here = pl.ds(part * 128, 128)
        for column, row in ((own_column, own_row), (other_column, other_row)):
            value = jnp.where(same, column[here, :].astype(f32), 0.0)
            row[:, here] = jnp.sum(value, axis=0, keepdims=True).astype(jnp.int32)

    for j in range(D // 128):
        d_wide[j] = d_encoded[:, j * 128 : (j + 1) * 128].astype(f32)
    place = lax.broadcasted_iota(jnp.int32, (LP, 1), 0)
    for first in range(0, USERS, 2):
        pair = []
        for u in (first, first + 1):
            rows = pl.ds(u, L, stride=USERS)
            one = jnp.concatenate([d_wide[j, rows, :] for j in range(D // 128)], axis=1)
            one = jnp.concatenate([one, jnp.zeros((LP - L, D), f32)], axis=0)
            pair.append(jnp.where(place < lens[u], one, 0.0))
        d_out[pl.ds(first * LP, 2 * LP), :] = jnp.concatenate(pair, axis=0).astype(bf16)
    for part in range(USERS // SUB):
        here = pl.ds(part * SUB_ROWS, SUB_ROWS)
        d_attended[here, :] = dot_nt(d_out[here, :], w_out[...]).astype(bf16)
    load.wait()


def run_prepare(core, lens, slots, requests, d_encoded, w_out, w_qkv, after):
    count = USERS * LP
    whole = lambda r, w, t: jax.ShapeDtypeStruct((r, w), t)
    return pl.pallas_call(
        prepare,
        in_specs=[SMEM, SMEM] + [VMEM] * 4 + [HBM, ANY],
        out_specs=[VMEM] * 7,
        out_shape=[
            pltpu.VMEM((count, D), bf16), pltpu.VMEM((count, D), bf16), whole(count, 1, jnp.int32), whole(count, 1, jnp.int32),
            whole(1, count, jnp.int32), whole(1, count, jnp.int32), pltpu.VMEM((D, 3 * D), bf16),
        ],
        scratch_shapes=[pltpu.VMEM((D // 128, USERS * L, 128), f32), pltpu.SemaphoreType.DMA],
        compiler_params=params(16),
        cost_estimate=cost(2 * count * D * D, 8 * count * D),
        name="prepare",
    )(core, lens, slots, requests, d_encoded, w_out, in_hbm(w_qkv), after)


def gather_own(index, table, out):
    at = lax.broadcasted_iota(jnp.int32, (ROWS, OWNERS * HALF), 1)
    out[...] = dot_nn((at == index[...]).astype(bf16), table[...]).astype(bf16)


def run_gather_own(index, table):
    part = lambda w: pl.BlockSpec((ROWS, w), lambda j: (j, 0))
    count = USERS * LP
    return pl.pallas_call(
        gather_own,
        grid=(USERS // GROUP,),
        in_specs=[part(1), VMEM],
        out_specs=part(D),
        out_shape=jax.ShapeDtypeStruct((count, D), bf16),
        compiler_params=params(12),
        cost_estimate=cost(2 * count * OWNERS * HALF * D, 6 * count * D),
        name="gather_own",
    )(index, table)


def encoder(lens, index, own_rows, table, pos, gain, w_qkv, w_out, d_out, d_attended, encoded, d_inputs):
    step = pl.program_id(0)
    at = lax.broadcasted_iota(jnp.int32, (ROWS, OWNERS * HALF), 1)
    x = dot_nn((at == index[...]).astype(bf16), table[...])
    x = x + own_rows[...].astype(f32)
    places = jnp.concatenate([pos[...].astype(f32), jnp.zeros((LP - L, D), f32)], axis=0)
    x = (x.reshape(GROUP, LP, D) + places[None]).reshape(ROWS, D)
    xhat, rstd = normalised(x)
    g = gain[...][None, :]
    packed = dot_nn((xhat * g).astype(bf16), w_qkv[...]).astype(bf16)

    subs = range(GROUP // SUB)
    cut = lambda value, sub: value[sub * SUB_ROWS : (sub + 1) * SUB_ROWS]
    join = lambda values: jnp.concatenate(values, axis=0)
    d_att = d_attended[...]
    q = [cut(packed[:, :D], sub) for sub in subs]
    k = [cut(packed[:, D : 2 * D], sub) for sub in subs]
    v = [cut(packed[:, 2 * D :], sub) for sub in subs]
    place = lax.broadcasted_iota(jnp.int32, (SUB_ROWS, 1), 0)
    column = lax.broadcasted_iota(jnp.int32, (SUB_ROWS, SUB_ROWS), 1)
    raw = [dot_nt(q[sub], k[sub]) for sub in subs]
    d_raw = [dot_nt(cut(d_att, sub), v[sub]) for sub in subs]
    live, probs16, d_scores = [], [], []
    for sub in subs:
        length = jnp.full((SUB_ROWS, 1), 0, jnp.int32)
        first = jnp.full((SUB_ROWS, 1), 0, jnp.int32)
        for u in range(SUB):
            here = (place >= u * LP) & (place < (u + 1) * LP)
            length = jnp.where(here, lens[step * GROUP + sub * SUB + u], length)
            first = jnp.where(here, u * LP, first)
        allowed = (column >= first) & (column <= place) & (column < first + length)
        live.append((place - first) < length)
        scores = jnp.where(allowed, raw[sub] / ROOT, MASKED)
        raised = jnp.exp(scores - jnp.max(scores, axis=-1, keepdims=True))
        probs = raised / jnp.sum(raised, axis=-1, keepdims=True)
        probs16.append(probs.astype(bf16))
        d_probs = d_raw[sub].astype(bf16).astype(f32)
        d_scores.append(
            (probs * (d_probs - jnp.sum(d_probs * probs, axis=-1, keepdims=True)) / ROOT).astype(bf16)
        )
    attended = join([dot_nn(probs16[sub], v[sub]).astype(bf16) for sub in subs])
    d_q = join([dot_nn(d_scores[sub], k[sub]).astype(bf16) for sub in subs])
    d_k = join([dot_tn(d_scores[sub], q[sub]).astype(bf16) for sub in subs])
    d_v = join([dot_tn(probs16[sub], cut(d_att, sub)).astype(bf16) for sub in subs])
    encoded[...] = jnp.where(join(live), x + dot_nn(attended, w_out[...]), 0.0).astype(bf16)
    d_normed = dot_nt(jnp.concatenate([d_q, d_k, d_v], axis=1), w_qkv[...]).astype(bf16).astype(f32)
    d_inputs[...] = (d_out[...].astype(f32) + norm_back(d_normed, g, xhat, rstd)).astype(bf16)


def run_encoder(lens, index, own_rows, table, pos, gain, w_qkv, w_out, d_out, d_attended):
    part = lambda w: pl.BlockSpec((ROWS, w), lambda j: (j, 0))
    count = USERS * LP
    return pl.pallas_call(
        encoder,
        grid=(USERS // GROUP,),
        in_specs=[
            SMEM, part(1), part(D), VMEM, VMEM, VMEM, VMEM, VMEM, part(D), part(D),
        ],
        out_specs=[part(D), part(D)],
        out_shape=[jax.ShapeDtypeStruct((count, D), bf16)] * 2,
        compiler_params=params(ENC_MB),
        name="user_encoder",
    )(lens, index, own_rows, table, pos, gain, in_vmem(w_qkv), w_out, in_vmem(d_out), in_vmem(d_attended))


def reorder(by_user, after, by_place, wide):
    for first in range(0, USERS, 2):
        pair = by_user[pl.ds(first * LP, 2 * LP), :].astype(f32)
        for k in range(2):
            for j in range(D // 128):
                one = pair[k * LP : k * LP + L, j * 128 : (j + 1) * 128]
                wide[j, pl.ds(first + k, L, stride=USERS), :] = one
    for j in range(D // 128):
        by_place[:, j * 128 : (j + 1) * 128] = wide[j].astype(bf16)


def run_reorder(by_user, after):
    return pl.pallas_call(
        reorder,
        in_specs=[VMEM, ANY],
        out_specs=VMEM,
        out_shape=jax.ShapeDtypeStruct((USERS * L, D), bf16),
        scratch_shapes=[pltpu.VMEM((D // 128, USERS * L, 128), f32)],
        compiler_params=params(12),
        cost_estimate=cost(USERS * L * D, 6 * USERS * L * D),
        name="reorder",
    )(by_user, after)


def add_owners(parts, out):
    total = parts[0].astype(f32)
    for o in range(1, OWNERS):
        total = total + parts[o].astype(f32)
    out[...] = total.astype(bf16)


def add_parts(a, b, c, d, after, out):
    out[...] = sum(part[...].astype(f32) for part in (a, b, c, d)).astype(bf16)


def scatter(index, rows, out):
    block = out.shape[0]
    row = lax.broadcasted_iota(jnp.int32, (block, USERS * LP), 0) + pl.program_id(0) * block
    out[...] = dot_nn((row == index[...]).astype(bf16), rows[...]).astype(bf16)


def scatter_more(index, rows, so_far, out):
    block = out.shape[0]
    row = lax.broadcasted_iota(jnp.int32, (block, USERS * LP), 0) + pl.program_id(0) * block
    total = dot_nn((row == index[...]).astype(bf16), rows[...])
    out[...] = (total + so_far[...].astype(f32)).astype(bf16)


def run_scatter(body, *operands):
    count = USERS * LP
    steps = 2
    part = pl.BlockSpec((OWNERS * HALF // steps, D), lambda j: (j, 0))
    return pl.pallas_call(
        body,
        grid=(steps,),
        in_specs=[VMEM, VMEM, part][: len(operands)],
        out_specs=part,
        out_shape=jax.ShapeDtypeStruct((OWNERS * HALF, D), bf16),
        compiler_params=params(12),
        cost_estimate=cost(2 * count * OWNERS * HALF * D, 6 * count * D),
        name=body.__name__,
    )(*operands)


def turn(up, down, after, up_t, down_t):
    for p in range(PARTS):
        cut = pl.ds(p * (HID // PARTS), HID // PARTS)
        up_t[cut, :] = up[:, cut].T
        down_t[:, cut] = down[cut, :].T


def run_turn(up, down, after):
    return pl.pallas_call(
        turn,
        in_specs=[VMEM, VMEM, ANY],
        out_specs=[VMEM] * 2,
        out_shape=[pltpu.VMEM((HID, D), bf16), pltpu.VMEM((D, HID), bf16)],
        compiler_params=params(8),
        cost_estimate=cost(HID * D, 8 * HID * D),
        name="turn",
    )(in_vmem(up), in_vmem(down), after)


def frame_backward(
    core, d_mine, d_other, pay_mine, pay_other, query, frames, framed, gain, slope, up, down,
    out,
):
    upper = core[0] == 1
    order = lambda a, b: jnp.concatenate([jnp.where(upper, b, a), jnp.where(upper, a, b)], axis=0)
    dp = order(d_mine[...], d_other[...]).astype(f32)
    pay = order(pay_mine[...], pay_other[...]).astype(f32)
    x = framed[...].astype(f32)
    q = query[...][None, :]
    top, whole = read_stats(pay)
    weight = jnp.exp(jnp.sum(x * q, axis=-1, keepdims=True) / ROOT - top) / whole
    cross = jnp.sum(dp * x, axis=-1, keepdims=True)
    own = jnp.sum(dp * pay[:, :D], axis=-1, keepdims=True)
    grad = weight * (dp + ((cross - own) / ROOT) * q)
    grad16 = grad.astype(bf16)
    width = HID // PARTS
    total = jnp.zeros(grad.shape, f32)
    for p in range(PARTS):
        cut = pl.ds(p * width, width)
        d_hidden = dot_nn(grad16, down[:, cut]).astype(bf16).astype(f32)
        d_a = (d_hidden * slope[:, cut].astype(f32)).astype(bf16)
        total = total + dot_nn(d_a, up[cut, :])
    xhat, rstd = normalised(frames[...].astype(f32))
    d_normed = total.astype(bf16).astype(f32)
    out[...] = (grad + norm_back(d_normed, gain[...][None, :], xhat, rstd)).astype(bf16)


def run_frame_backward(core, d_mine, d_other, pay_mine, pay_other, query, frames, framed, gain, slope, w_up, w_down):
    rows = frames.shape[0]
    return pl.pallas_call(
        frame_backward,
        in_specs=[SMEM] + [VMEM] * 11,
        out_specs=VMEM,
        out_shape=jax.ShapeDtypeStruct((rows, D), bf16),
        compiler_params=params(FRAME_MB),
        name="frame_backward",
    )(core, d_mine, d_other, pay_mine, pay_other, query, frames, framed, gain, slope, in_vmem(w_up), in_vmem(w_down))


def swap_with(x, bits):
    pairs = [(i, i ^ bits) for i in range(8)]
    return lax.ppermute(x, "frame", pairs)


def spread_along_x(x):
    return [swap_with(x, 2 * k) for k in (1, 2, 3)]


def shards(
    frames, frame_gain, w_up, w_down, pool_query, pos_embed, user_gain, w_qkv, w_out,
    request_rows, hist_slot, hist_len, d_encoded,
):
    rows = frames.shape[0]
    c = lax.axis_index("frame") % 2
    core = c.astype(jnp.int32).reshape(1)
    flat_frames = frames.reshape(rows, D)
    gain = frame_gain
    query = pool_query

    mine, other, framed, slope, up, down = run_frame_forward(core, flat_frames, gain, w_up, w_down)
    theirs = swap_with(other, 1)
    payload = jax.ShapeDtypeStruct((HALF, PAY), bf16)
    pair = pl.pallas_call(
        pool_pair, in_specs=[VMEM] * 3, out_specs=VMEM, out_shape=payload, compiler_params=params(8), name="pool_pair",
    )(mine, theirs, query)
    cotangent = jnp.transpose(d_encoded, (1, 0, 2)).reshape(USERS * L, D)
    d_out, d_attended, own_column, other_column, own_row, other_row, qkv = run_prepare(
        core, hist_len, hist_slot, request_rows, cotangent, w_out, w_qkv, pair
    )
    up_turned, down_turned = run_turn(up, down, pair)
    early = (in_vmem(d_out), in_vmem(up_turned))
    spread, pay_mine = pl.pallas_call(
        pool_all, in_specs=[VMEM] * 4 + [pl.BlockSpec(memory_space=pl.ANY)] * len(early), out_specs=[VMEM] * 2,
        out_shape=[jax.ShapeDtypeStruct((OWNERS, HALF, D), bf16), payload], compiler_params=params(8), name="pool_all",
    )(pair, *spread_along_x(pair), *early)
    table = lax.all_to_all(spread, "dp", split_axis=0, concat_axis=0, tiled=True).reshape(OWNERS * HALF, D)
    other_table = swap_with(table, 1)
    own_rows = run_gather_own(own_column, table)
    encoded, d_inputs = run_encoder(
        hist_len, other_column, own_rows, other_table, pos_embed, user_gain, qkv, w_out, d_out, d_attended
    )
    peer_rows = swap_with(d_inputs, 1)
    peer_index = swap_with(other_row, 1)
    pay_other = swap_with(pay_mine, 1)
    d_table = run_scatter(scatter, own_row, d_inputs)
    d_table = run_scatter(scatter_more, peer_index, peer_rows, d_table)
    returned = lax.all_to_all(
        d_table.reshape(OWNERS, HALF, D), "dp", split_axis=0, concat_axis=0, tiled=True
    )
    partial = pl.pallas_call(
        add_owners, in_specs=[VMEM], out_specs=VMEM, out_shape=jax.ShapeDtypeStruct((HALF, D), bf16),
        compiler_params=params(8), name="add_owners",
    )(returned)
    encoded = run_reorder(encoded, partial)
    d_mine = pl.pallas_call(
        add_parts, in_specs=[VMEM] * 4 + [ANY], out_specs=VMEM, out_shape=jax.ShapeDtypeStruct((HALF, D), bf16),
        compiler_params=params(8), name="add_parts",
    )(partial, *spread_along_x(partial), in_hbm(encoded))
    d_other = swap_with(d_mine, 1)
    d_frames = run_frame_backward(
        core, d_mine, d_other, pay_mine, pay_other, query, flat_frames, framed, gain, slope, up_turned, down_turned
    )
    encoded = jnp.transpose(encoded.reshape(L, USERS, D), (1, 0, 2))
    return encoded, d_frames.reshape(rows, 1, D)


def solution(mesh):
    in_specs = (
        P("dp", "frame", None),
        P(),
        P(),
        P(),
        P(),
        P(),
        P(),
        P(),
        P(),
        P(("dp", "frame"), None, None),
        P(("dp", "frame"), None),
        P(("dp", "frame")),
        P(("dp", "frame"), None, None),
    )
    out_specs = (P(("dp", "frame"), None, None), P("dp", "frame", None))
    return jax.shard_map(shards, mesh=mesh, in_specs=in_specs, out_specs=out_specs, check_vma=False)
```

```python
import functools
import math

import jax
import jax.numpy as jnp
from jax import lax
from jax.experimental import pallas as pl
from jax.experimental.pallas import tpu as pltpu
from jax.sharding import PartitionSpec as P

D = 768
HID = 3072
L = 50
LP = 56
USERS = 16
GROUP = 16
ROWS = GROUP * LP
SUB = 4
SUB_ROWS = SUB * LP
ENC_MB = 36
OWNERS = 16
HALF = 64
CAP = 64
PAY = D + 128
EPS = 1e-6
ROOT = math.sqrt(D)
MASKED = -1e9
AXES = ("dp", "frame")
f32 = jnp.float32
bf16 = jnp.bfloat16
VMEM = pl.BlockSpec(memory_space=pltpu.VMEM)
SMEM = pl.BlockSpec(memory_space=pltpu.SMEM)
ANY = pl.BlockSpec(memory_space=pl.ANY)
HBM = pl.BlockSpec(memory_space=pltpu.HBM)
PARTS = 4
FRAME_MB = 16


def dot_nn(a, b):
    return lax.dot_general(a, b, (((1,), (0,)), ((), ())), preferred_element_type=f32)


def dot_nt(a, b):
    return lax.dot_general(a, b, (((1,), (1,)), ((), ())), preferred_element_type=f32)


def dot_tn(a, b):
    return lax.dot_general(a, b, (((0,), (0,)), ((), ())), preferred_element_type=f32)


def in_vmem(x):
    return pltpu.with_memory_space_constraint(x, pltpu.VMEM)


def in_hbm(x):
    return pltpu.with_memory_space_constraint(x, pltpu.HBM)


def params(megabytes):
    return pltpu.CompilerParams(vmem_limit_bytes=megabytes << 20)


def cost(flops, moved):
    return pl.CostEstimate(flops=int(flops), bytes_accessed=int(moved), transcendentals=0)


def normalised(x):
    centred = x - jnp.mean(x, axis=-1, keepdims=True)
    rstd = lax.rsqrt(jnp.mean(centred * centred, axis=-1, keepdims=True) + EPS)
    return centred * rstd, rstd


def norm_back(d_normed, gain, xhat, rstd):
    d_hat = d_normed * gain
    along = jnp.mean(d_hat * xhat, axis=-1, keepdims=True)
    return rstd * (d_hat - jnp.mean(d_hat, axis=-1, keepdims=True) - xhat * along)


def fetch(source, target, sems, axis, parts):
    width = source.shape[axis] // parts
    copies = []
    for p in range(parts):
        cut = pl.ds(p * width, width)
        where = (cut, slice(None)) if axis == 0 else (slice(None), cut)
        copies.append(pltpu.make_async_copy(source.at[where], target.at[where], sems.at[p]))
    return copies


def frame_forward(
    core, frames_in, gain_in, w_up, w_down, mine, other, out, slope, up, down, frames, gain, sems, up_sems, down_sems
):
    first = [pltpu.make_async_copy(frames_in, frames, sems.at[0]), pltpu.make_async_copy(gain_in, gain, sems.at[1])]
    for one in first:
        one.start()
    ups = fetch(w_up, up, up_sems, 1, PARTS)
    downs = fetch(w_down, down, down_sems, 0, PARTS)
    for one, two in zip(ups, downs):
        one.start()
        two.start()
    for one in first:
        one.wait()
    x = frames[...].astype(f32)
    xhat, _ = normalised(x)
    normed = (xhat * gain[...][None, :]).astype(bf16)
    total = x
    width = HID // PARTS
    c0 = math.sqrt(2.0 / math.pi)
    for p in range(PARTS):
        cut = pl.ds(p * width, width)
        ups[p].wait()
        a = dot_nn(normed, up[:, cut])
        square = a * a
        th = jnp.tanh(c0 * a * (1.0 + 0.044715 * square))
        half = 0.5 * (1.0 + th)
        hidden = (a * half).astype(bf16)
        slope[:, cut] = (half + 0.5 * a * (1.0 - th * th) * c0 * (1.0 + 3 * 0.044715 * square)).astype(bf16)
        downs[p].wait()
        total = total + dot_nn(hidden, down[cut, :])
    stored = total.astype(bf16)
    out[...] = stored
    upper = core[0] == 1
    mine[...] = jnp.where(upper, stored[HALF:], stored[:HALF])
    other[...] = jnp.where(upper, stored[:HALF], stored[HALF:])


def run_frame_forward(core, frames, gain, w_up, w_down):
    rows = frames.shape[0]
    return pl.pallas_call(
        frame_forward,
        in_specs=[SMEM, HBM, HBM, HBM, HBM],
        out_specs=[VMEM] * 6,
        out_shape=[
            jax.ShapeDtypeStruct((HALF, D), bf16),
            jax.ShapeDtypeStruct((HALF, D), bf16),
            jax.ShapeDtypeStruct((rows, D), bf16),
            jax.ShapeDtypeStruct((rows, HID), bf16),
            pltpu.VMEM((D, HID), bf16),
            pltpu.VMEM((HID, D), bf16),
        ],
        scratch_shapes=[
            pltpu.VMEM((rows, D), bf16), pltpu.VMEM((D,), f32), pltpu.SemaphoreType.DMA((2,)),
            pltpu.SemaphoreType.DMA((PARTS,)), pltpu.SemaphoreType.DMA((PARTS,)),
        ],
        compiler_params=params(FRAME_MB),
        name="frame_forward",
    )(core, in_hbm(frames), in_hbm(gain), in_hbm(w_up), in_hbm(w_down))


def pieces(value):
    first = value.astype(bf16).astype(f32)
    rest = value - first
    second = rest.astype(bf16).astype(f32)
    return first, second, rest - second


def write_payload(out, mean, top, total):
    lane = lax.broadcasted_iota(jnp.int32, (HALF, 128), 1)
    stats = jnp.zeros((HALF, 128), f32)
    for at, piece in enumerate(pieces(top) + pieces(total)):
        stats = jnp.where(lane == at, piece, stats)
    out[:, :D] = mean.astype(bf16)
    out[:, D:] = stats.astype(bf16)


def read_stats(block):
    stats = block[:, D:].astype(f32)
    lane = lax.broadcasted_iota(jnp.int32, stats.shape, 1)
    top = jnp.sum(jnp.where(lane < 3, stats, 0.0), axis=-1, keepdims=True)
    total = jnp.sum(jnp.where((lane >= 3) & (lane < 6), stats, 0.0), axis=-1, keepdims=True)
    return top, total


def pool_pair(mine, theirs, query, out):
    a = mine[...].astype(f32)
    b = theirs[...].astype(f32)
    q = query[...][None, :]
    score_a = jnp.sum(a * q, axis=-1, keepdims=True) / ROOT
    score_b = jnp.sum(b * q, axis=-1, keepdims=True) / ROOT
    top = jnp.maximum(score_a, score_b)
    weight_a = jnp.exp(score_a - top)
    weight_b = jnp.exp(score_b - top)
    total = weight_a + weight_b
    write_payload(out, (weight_a * a + weight_b * b) / total, top, total)


def pool_all(p0, p1, p2, p3, *rest):
    spread, out = rest[-2:]
    parts = (p0, p1, p2, p3)
    stats = [read_stats(p) for p in parts]
    top = functools.reduce(jnp.maximum, [s[0] for s in stats])
    weights = [jnp.exp(s[0] - top) * s[1] for s in stats]
    total = sum(weights)
    mean = sum(w * p[:, :D].astype(f32) for w, p in zip(weights, parts)) / total
    write_payload(out, mean, top, total)
    rows = mean.astype(bf16)
    for o in range(OWNERS):
        spread[o] = rows


def prepare(
    core, lens, slots, requests, d_encoded, w_out, w_qkv, after,
    d_out, d_attended, own_column, other_column, own_row, other_row, qkv, d_wide, sem,
):
    load = pltpu.make_async_copy(w_qkv, qkv, sem)
    load.start()
    c = core[0]
    lane = lax.broadcasted_iota(jnp.int32, (LP, L), 1)
    diagonal = lane == lax.broadcasted_iota(jnp.int32, (LP, L), 0)
    inside = lax.broadcasted_iota(jnp.int32, (LP, 1), 0) < L
    owner_lane = lax.broadcasted_iota(jnp.int32, (LP, OWNERS), 1)
    cap_lane = lax.broadcasted_iota(jnp.int32, (LP, CAP), 1)
    asked = requests[0].astype(f32).astype(bf16)
    for u in range(USERS):
        slot = jnp.sum(jnp.where(diagonal, slots[u : u + 1, :].astype(f32), 0.0), axis=1, keepdims=True)
        slot = slot.astype(jnp.int32)
        owner = slot >> 6
        lists = dot_nn((owner_lane == owner).astype(bf16), asked)
        local = jnp.sum(jnp.where(cap_lane == (slot & (CAP - 1)), lists, 0.0), axis=1, keepdims=True)
        local = local.astype(jnp.int32)
        position = jnp.where(inside, owner * HALF + (local & (HALF - 1)), -1)
        own = (local >> 6) == c
        here = pl.ds(u * LP, LP)
        own_column[here, :] = jnp.where(own, position, -1)
        other_column[here, :] = jnp.where(own, -1, position)
    square = (128, 128)
    same = lax.broadcasted_iota(jnp.int32, square, 0) == lax.broadcasted_iota(jnp.int32, square, 1)
    for part in range(USERS * LP // 128):
        here = pl.ds(part * 128, 128)
        for column, row in ((own_column, own_row), (other_column, other_row)):
            value = jnp.where(same, column[here, :].astype(f32), 0.0)
            row[:, here] = jnp.sum(value, axis=0, keepdims=True).astype(jnp.int32)

    for j in range(D // 128):
        d_wide[j] = d_encoded[:, j * 128 : (j + 1) * 128].astype(f32)
    place = lax.broadcasted_iota(jnp.int32, (LP, 1), 0)
    for first in range(0, USERS, 2):
        pair = []
        for u in (first, first + 1):
            rows = pl.ds(u, L, stride=USERS)
            one = jnp.concatenate([d_wide[j, rows, :] for j in range(D // 128)], axis=1)
            one = jnp.concatenate([one, jnp.zeros((LP - L, D), f32)], axis=0)
            pair.append(jnp.where(place < lens[u], one, 0.0))
        d_out[pl.ds(first * LP, 2 * LP), :] = jnp.concatenate(pair, axis=0).astype(bf16)
    for part in range(USERS // SUB):
        here = pl.ds(part * SUB_ROWS, SUB_ROWS)
        d_attended[here, :] = dot_nt(d_out[here, :], w_out[...]).astype(bf16)
    load.wait()


def run_prepare(core, lens, slots, requests, d_encoded, w_out, w_qkv, after):
    count = USERS * LP
    whole = lambda r, w, t: jax.ShapeDtypeStruct((r, w), t)
    return pl.pallas_call(
        prepare,
        in_specs=[SMEM, SMEM] + [VMEM] * 4 + [HBM, ANY],
        out_specs=[VMEM] * 7,
        out_shape=[
            pltpu.VMEM((count, D), bf16), pltpu.VMEM((count, D), bf16), whole(count, 1, jnp.int32), whole(count, 1, jnp.int32),
            whole(1, count, jnp.int32), whole(1, count, jnp.int32), pltpu.VMEM((D, 3 * D), bf16),
        ],
        scratch_shapes=[pltpu.VMEM((D // 128, USERS * L, 128), f32), pltpu.SemaphoreType.DMA],
        compiler_params=params(16),
        cost_estimate=cost(2 * count * D * D, 8 * count * D),
        name="prepare",
    )(core, lens, slots, requests, d_encoded, w_out, in_hbm(w_qkv), after)


def gather_own(index, table, out):
    at = lax.broadcasted_iota(jnp.int32, (ROWS, OWNERS * HALF), 1)
    out[...] = dot_nn((at == index[...]).astype(bf16), table[...]).astype(bf16)


def run_gather_own(index, table):
    part = lambda w: pl.BlockSpec((ROWS, w), lambda j: (j, 0))
    count = USERS * LP
    return pl.pallas_call(
        gather_own,
        grid=(USERS // GROUP,),
        in_specs=[part(1), VMEM],
        out_specs=part(D),
        out_shape=jax.ShapeDtypeStruct((count, D), bf16),
        compiler_params=params(12),
        cost_estimate=cost(2 * count * OWNERS * HALF * D, 6 * count * D),
        name="gather_own",
    )(index, table)


def encoder(
    lens, index, own_rows, table, pos, gain, w_qkv, w_out, d_out, d_attended, *rest
):
    encoded, d_inputs = rest[-2:]
    step = pl.program_id(0)
    some = ROWS // 2
    at = lax.broadcasted_iota(jnp.int32, (some, OWNERS * HALF), 1)
    places = jnp.concatenate([pos[...].astype(f32), jnp.zeros((LP - L, D), f32)], axis=0)
    g = gain[...][None, :]
    xs, xhats, rstds, packs = [], [], [], []
    for part in range(2):
        here = pl.ds(part * some, some)
        x = dot_nn((at == index[here, :]).astype(bf16), table[...])
        x = x + own_rows[here, :].astype(f32)
        x = (x.reshape(some // LP, LP, D) + places[None]).reshape(some, D)
        xs.append(x)
    for x in xs:
        xhat, rstd = normalised(x)
        xhats.append(xhat)
        rstds.append(rstd)
        packs.append(dot_nn((xhat * g).astype(bf16), w_qkv[...]).astype(bf16))
    x, xhat, rstd, packed = [jnp.concatenate(v, axis=0) for v in (xs, xhats, rstds, packs)]

    subs = range(GROUP // SUB)
    cut = lambda value, sub: value[sub * SUB_ROWS : (sub + 1) * SUB_ROWS]
    join = lambda values: jnp.concatenate(values, axis=0)
    d_att = d_attended[...]
    q = [cut(packed[:, :D], sub) for sub in subs]
    k = [cut(packed[:, D : 2 * D], sub) for sub in subs]
    v = [cut(packed[:, 2 * D :], sub) for sub in subs]
    place = lax.broadcasted_iota(jnp.int32, (SUB_ROWS, 1), 0)
    column = lax.broadcasted_iota(jnp.int32, (SUB_ROWS, SUB_ROWS), 1)
    raw = [dot_nt(q[sub], k[sub]) for sub in subs]
    d_raw = [dot_nt(cut(d_att, sub), v[sub]) for sub in subs]
    live, probs16, d_scores = [], [], []
    for sub in subs:
        length = jnp.full((SUB_ROWS, 1), 0, jnp.int32)
        first = jnp.full((SUB_ROWS, 1), 0, jnp.int32)
        for u in range(SUB):
            here = (place >= u * LP) & (place < (u + 1) * LP)
            length = jnp.where(here, lens[step * GROUP + sub * SUB + u], length)
            first = jnp.where(here, u * LP, first)
        allowed = (column >= first) & (column <= place) & (column < first + length)
        live.append((place - first) < length)
        scores = jnp.where(allowed, raw[sub] / ROOT, MASKED)
        raised = jnp.exp(scores - jnp.max(scores, axis=-1, keepdims=True))
        probs = raised / jnp.sum(raised, axis=-1, keepdims=True)
        probs16.append(probs.astype(bf16))
        d_probs = d_raw[sub].astype(bf16).astype(f32)
        d_scores.append(
            (probs * (d_probs - jnp.sum(d_probs * probs, axis=-1, keepdims=True)) / ROOT).astype(bf16)
        )
    attended = join([dot_nn(probs16[sub], v[sub]).astype(bf16) for sub in subs])
    d_q = join([dot_nn(d_scores[sub], k[sub]).astype(bf16) for sub in subs])
    d_k = join([dot_tn(d_scores[sub], q[sub]).astype(bf16) for sub in subs])
    d_v = join([dot_tn(probs16[sub], cut(d_att, sub)).astype(bf16) for sub in subs])
    encoded[...] = jnp.where(join(live), x + dot_nn(attended, w_out[...]), 0.0).astype(bf16)
    joined = jnp.concatenate([d_q, d_k, d_v], axis=1)
    step_rows = ROWS // 2
    for part in range(2):
        lo, hi = part * step_rows, (part + 1) * step_rows
        d_normed = dot_nt(joined[lo:hi], w_qkv[...]).astype(bf16).astype(f32)
        back = norm_back(d_normed, g, xhat[lo:hi], rstd[lo:hi])
        d_inputs[lo:hi, :] = (d_out[lo:hi, :].astype(f32) + back).astype(bf16)


def run_encoder(lens, index, own_rows, table, pos, gain, w_qkv, w_out, d_out, d_attended, early):
    part = lambda w: pl.BlockSpec((ROWS, w), lambda j: (j, 0))
    count = USERS * LP
    return pl.pallas_call(
        encoder,
        grid=(USERS // GROUP,),
        in_specs=[
            SMEM, part(1), part(D), VMEM, VMEM, VMEM, VMEM, VMEM, part(D), part(D),
            *[ANY] * len(early),
        ],
        out_specs=[part(D), part(D)],
        out_shape=[jax.ShapeDtypeStruct((count, D), bf16)] * 2,
        compiler_params=params(ENC_MB),
        name="user_encoder",
    )(lens, index, own_rows, table, pos, gain, in_vmem(w_qkv), w_out, in_vmem(d_out), in_vmem(d_attended), *[in_vmem(x) for x in early])


def reorder(by_user, after, by_place, wide):
    for first in range(0, USERS, 2):
        pair = by_user[pl.ds(first * LP, 2 * LP), :].astype(f32)
        for k in range(2):
            for j in range(D // 128):
                one = pair[k * LP : k * LP + L, j * 128 : (j + 1) * 128]
                wide[j, pl.ds(first + k, L, stride=USERS), :] = one
    for j in range(D // 128):
        by_place[:, j * 128 : (j + 1) * 128] = wide[j].astype(bf16)


def run_reorder(by_user, after):
    return pl.pallas_call(
        reorder,
        in_specs=[VMEM, ANY],
        out_specs=VMEM,
        out_shape=jax.ShapeDtypeStruct((USERS * L, D), bf16),
        scratch_shapes=[pltpu.VMEM((D // 128, USERS * L, 128), f32)],
        compiler_params=params(12),
        cost_estimate=cost(USERS * L * D, 6 * USERS * L * D),
        name="reorder",
    )(by_user, after)


def add_owners(parts, out):
    total = parts[0].astype(f32)
    for o in range(1, OWNERS):
        total = total + parts[o].astype(f32)
    out[...] = total.astype(bf16)


def add_parts(a, b, c, d, after, out):
    out[...] = sum(part[...].astype(f32) for part in (a, b, c, d)).astype(bf16)


def scatter(index, rows, out):
    block = out.shape[0]
    row = lax.broadcasted_iota(jnp.int32, (block, USERS * LP), 0) + pl.program_id(0) * block
    out[...] = dot_nn((row == index[...]).astype(bf16), rows[...]).astype(bf16)


def scatter_more(index, rows, so_far, out):
    block = out.shape[0]
    row = lax.broadcasted_iota(jnp.int32, (block, USERS * LP), 0) + pl.program_id(0) * block
    total = dot_nn((row == index[...]).astype(bf16), rows[...])
    out[...] = (total + so_far[...].astype(f32)).astype(bf16)


def run_scatter(body, *operands):
    count = USERS * LP
    steps = 2
    part = pl.BlockSpec((OWNERS * HALF // steps, D), lambda j: (j, 0))
    return pl.pallas_call(
        body,
        grid=(steps,),
        in_specs=[VMEM, VMEM, part][: len(operands)],
        out_specs=part,
        out_shape=jax.ShapeDtypeStruct((OWNERS * HALF, D), bf16),
        compiler_params=params(12),
        cost_estimate=cost(2 * count * OWNERS * HALF * D, 6 * count * D),
        name=body.__name__,
    )(*operands)


def turn(up, down, after, up_t, down_t):
    for p in range(PARTS):
        cut = pl.ds(p * (HID // PARTS), HID // PARTS)
        up_t[cut, :] = up[:, cut].T
        down_t[:, cut] = down[cut, :].T


def run_turn(up, down, after):
    return pl.pallas_call(
        turn,
        in_specs=[VMEM, VMEM, ANY],
        out_specs=[VMEM] * 2,
        out_shape=[pltpu.VMEM((HID, D), bf16), pltpu.VMEM((D, HID), bf16)],
        compiler_params=params(8),
        cost_estimate=cost(HID * D, 8 * HID * D),
        name="turn",
    )(in_vmem(up), in_vmem(down), after)


def frame_backward(
    core, d_mine, d_other, pay_mine, pay_other, query, frames, framed, gain, slope, up, down,
    out,
):
    upper = core[0] == 1
    order = lambda a, b: jnp.concatenate([jnp.where(upper, b, a), jnp.where(upper, a, b)], axis=0)
    dp = order(d_mine[...], d_other[...]).astype(f32)
    pay = order(pay_mine[...], pay_other[...]).astype(f32)
    x = framed[...].astype(f32)
    q = query[...][None, :]
    top, whole = read_stats(pay)
    weight = jnp.exp(jnp.sum(x * q, axis=-1, keepdims=True) / ROOT - top) / whole
    cross = jnp.sum(dp * x, axis=-1, keepdims=True)
    own = jnp.sum(dp * pay[:, :D], axis=-1, keepdims=True)
    grad = weight * (dp + ((cross - own) / ROOT) * q)
    grad16 = grad.astype(bf16)
    width = HID // PARTS
    total = jnp.zeros(grad.shape, f32)
    for p in range(PARTS):
        cut = pl.ds(p * width, width)
        d_hidden = dot_nn(grad16, down[:, cut]).astype(bf16).astype(f32)
        d_a = (d_hidden * slope[:, cut].astype(f32)).astype(bf16)
        total = total + dot_nn(d_a, up[cut, :])
    xhat, rstd = normalised(frames[...].astype(f32))
    d_normed = total.astype(bf16).astype(f32)
    out[...] = (grad + norm_back(d_normed, gain[...][None, :], xhat, rstd)).astype(bf16)


def run_frame_backward(core, d_mine, d_other, pay_mine, pay_other, query, frames, framed, gain, slope, w_up, w_down):
    rows = frames.shape[0]
    return pl.pallas_call(
        frame_backward,
        in_specs=[SMEM] + [VMEM] * 11,
        out_specs=VMEM,
        out_shape=jax.ShapeDtypeStruct((rows, D), bf16),
        compiler_params=params(FRAME_MB),
        name="frame_backward",
    )(core, d_mine, d_other, pay_mine, pay_other, query, frames, framed, gain, slope, in_vmem(w_up), in_vmem(w_down))


def swap_with(x, bits):
    pairs = [(i, i ^ bits) for i in range(8)]
    return lax.ppermute(x, "frame", pairs)


def spread_along_x(x):
    return [swap_with(x, 2 * k) for k in (1, 2, 3)]


def shards(
    frames, frame_gain, w_up, w_down, pool_query, pos_embed, user_gain, w_qkv, w_out,
    request_rows, hist_slot, hist_len, d_encoded,
):
    rows = frames.shape[0]
    c = lax.axis_index("frame") % 2
    core = c.astype(jnp.int32).reshape(1)
    flat_frames = frames.reshape(rows, D)
    gain = frame_gain
    query = pool_query

    mine, other, framed, slope, up, down = run_frame_forward(core, flat_frames, gain, w_up, w_down)
    theirs = swap_with(other, 1)
    payload = jax.ShapeDtypeStruct((HALF, PAY), bf16)
    pair = pl.pallas_call(
        pool_pair, in_specs=[VMEM] * 3, out_specs=VMEM, out_shape=payload, compiler_params=params(8), name="pool_pair",
    )(mine, theirs, query)
    cotangent = jnp.transpose(d_encoded, (1, 0, 2)).reshape(USERS * L, D)
    d_out, d_attended, own_column, other_column, own_row, other_row, qkv = run_prepare(
        core, hist_len, hist_slot, request_rows, cotangent, w_out, w_qkv, pair
    )
    up_turned, down_turned = run_turn(up, down, pair)
    early = (in_vmem(d_out), in_vmem(up_turned))
    spread, pay_mine = pl.pallas_call(
        pool_all, in_specs=[VMEM] * 4 + [pl.BlockSpec(memory_space=pl.ANY)] * len(early), out_specs=[VMEM] * 2,
        out_shape=[jax.ShapeDtypeStruct((OWNERS, HALF, D), bf16), payload], compiler_params=params(8), name="pool_all",
    )(pair, *spread_along_x(pair), *early)
    table = lax.all_to_all(spread, "dp", split_axis=0, concat_axis=0, tiled=True).reshape(OWNERS * HALF, D)
    other_table = swap_with(table, 1)
    own_rows = run_gather_own(own_column, table)
    peer_index = swap_with(other_row, 1)
    pay_other = swap_with(pay_mine, 1)
    encoded, d_inputs = run_encoder(
        hist_len, other_column, own_rows, other_table, pos_embed, user_gain, qkv, w_out, d_out, d_attended,
        (peer_index, pay_other),
    )
    peer_rows = swap_with(d_inputs, 1)
    d_table = run_scatter(scatter, own_row, d_inputs)
    d_table = run_scatter(scatter_more, peer_index, peer_rows, d_table)
    returned = lax.all_to_all(
        d_table.reshape(OWNERS, HALF, D), "dp", split_axis=0, concat_axis=0, tiled=True
    )
    partial = pl.pallas_call(
        add_owners, in_specs=[VMEM], out_specs=VMEM, out_shape=jax.ShapeDtypeStruct((HALF, D), bf16),
        compiler_params=params(8), name="add_owners",
    )(returned)
    encoded = run_reorder(encoded, partial)
    d_mine = pl.pallas_call(
        add_parts, in_specs=[VMEM] * 4 + [ANY], out_specs=VMEM, out_shape=jax.ShapeDtypeStruct((HALF, D), bf16),
        compiler_params=params(8), name="add_parts",
    )(partial, *spread_along_x(partial), in_hbm(encoded))
    d_other = swap_with(d_mine, 1)
    d_frames = run_frame_backward(
        core, d_mine, d_other, pay_mine, pay_other, query, flat_frames, framed, gain, slope, up_turned, down_turned
    )
    encoded = jnp.transpose(encoded.reshape(L, USERS, D), (1, 0, 2))
    return encoded, d_frames.reshape(rows, 1, D)


def solution(mesh):
    in_specs = (
        P("dp", "frame", None),
        P(),
        P(),
        P(),
        P(),
        P(),
        P(),
        P(),
        P(),
        P(("dp", "frame"), None, None),
        P(("dp", "frame"), None),
        P(("dp", "frame")),
        P(("dp", "frame"), None, None),
    )
    out_specs = (P(("dp", "frame"), None, None), P("dp", "frame", None))
    return jax.shard_map(shards, mesh=mesh, in_specs=in_specs, out_specs=out_specs, check_vma=False)
```

```python
import functools
import math

import jax
import jax.numpy as jnp
from jax import lax
from jax.experimental import pallas as pl
from jax.experimental.pallas import tpu as pltpu
from jax.sharding import PartitionSpec as P

D = 768
HID = 3072
L = 50
LP = 56
USERS = 16
GROUP = 16
ROWS = GROUP * LP
SUB = 4
SUB_ROWS = SUB * LP
ENC_MB = 36
PART = USERS * LP // 2
LANES = 512
OWNERS = 16
HALF = 64
CAP = 64
PAY = D + 128
EPS = 1e-6
ROOT = math.sqrt(D)
MASKED = -1e9
AXES = ("dp", "frame")
f32 = jnp.float32
bf16 = jnp.bfloat16
VMEM = pl.BlockSpec(memory_space=pltpu.VMEM)
SMEM = pl.BlockSpec(memory_space=pltpu.SMEM)
ANY = pl.BlockSpec(memory_space=pl.ANY)
HBM = pl.BlockSpec(memory_space=pltpu.HBM)
PARTS = 4
FRAME_MB = 16


def dot_nn(a, b):
    return lax.dot_general(a, b, (((1,), (0,)), ((), ())), preferred_element_type=f32)


def dot_nt(a, b):
    return lax.dot_general(a, b, (((1,), (1,)), ((), ())), preferred_element_type=f32)


def dot_tn(a, b):
    return lax.dot_general(a, b, (((0,), (0,)), ((), ())), preferred_element_type=f32)


def in_vmem(x):
    return pltpu.with_memory_space_constraint(x, pltpu.VMEM)


def in_hbm(x):
    return pltpu.with_memory_space_constraint(x, pltpu.HBM)


def params(megabytes):
    return pltpu.CompilerParams(vmem_limit_bytes=megabytes << 20)


def cost(flops, moved):
    return pl.CostEstimate(flops=int(flops), bytes_accessed=int(moved), transcendentals=0)


def normalised(x):
    centred = x - jnp.mean(x, axis=-1, keepdims=True)
    rstd = lax.rsqrt(jnp.mean(centred * centred, axis=-1, keepdims=True) + EPS)
    return centred * rstd, rstd


def norm_back(d_normed, gain, xhat, rstd):
    d_hat = d_normed * gain
    along = jnp.mean(d_hat * xhat, axis=-1, keepdims=True)
    return rstd * (d_hat - jnp.mean(d_hat, axis=-1, keepdims=True) - xhat * along)


def fetch(source, target, sems, axis, parts):
    width = source.shape[axis] // parts
    copies = []
    for p in range(parts):
        cut = pl.ds(p * width, width)
        where = (cut, slice(None)) if axis == 0 else (slice(None), cut)
        copies.append(pltpu.make_async_copy(source.at[where], target.at[where], sems.at[p]))
    return copies


def frame_forward(
    core, frames_in, gain_in, w_up, w_down, mine, other, out, slope, up, down, frames, gain, sems, up_sems, down_sems
):
    first = [pltpu.make_async_copy(frames_in, frames, sems.at[0]), pltpu.make_async_copy(gain_in, gain, sems.at[1])]
    for one in first:
        one.start()
    ups = fetch(w_up, up, up_sems, 1, PARTS)
    downs = fetch(w_down, down, down_sems, 0, PARTS)
    for one, two in zip(ups, downs):
        one.start()
        two.start()
    for one in first:
        one.wait()
    x = frames[...].astype(f32)
    xhat, _ = normalised(x)
    normed = (xhat * gain[...][None, :]).astype(bf16)
    total = x
    width = HID // PARTS
    c0 = math.sqrt(2.0 / math.pi)
    for p in range(PARTS):
        cut = pl.ds(p * width, width)
        ups[p].wait()
        a = dot_nn(normed, up[:, cut])
        square = a * a
        th = jnp.tanh(c0 * a * (1.0 + 0.044715 * square))
        half = 0.5 * (1.0 + th)
        hidden = (a * half).astype(bf16)
        slope[:, cut] = (half + 0.5 * a * (1.0 - th * th) * c0 * (1.0 + 3 * 0.044715 * square)).astype(bf16)
        downs[p].wait()
        total = total + dot_nn(hidden, down[cut, :])
    stored = total.astype(bf16)
    out[...] = stored
    upper = core[0] == 1
    mine[...] = jnp.where(upper, stored[HALF:], stored[:HALF])
    other[...] = jnp.where(upper, stored[:HALF], stored[HALF:])


def run_frame_forward(core, frames, gain, w_up, w_down):
    rows = frames.shape[0]
    return pl.pallas_call(
        frame_forward,
        in_specs=[SMEM, HBM, HBM, HBM, HBM],
        out_specs=[VMEM] * 6,
        out_shape=[
            jax.ShapeDtypeStruct((HALF, D), bf16),
            jax.ShapeDtypeStruct((HALF, D), bf16),
            jax.ShapeDtypeStruct((rows, D), bf16),
            jax.ShapeDtypeStruct((rows, HID), bf16),
            pltpu.VMEM((D, HID), bf16),
            pltpu.VMEM((HID, D), bf16),
        ],
        scratch_shapes=[
            pltpu.VMEM((rows, D), bf16), pltpu.VMEM((D,), f32), pltpu.SemaphoreType.DMA((2,)),
            pltpu.SemaphoreType.DMA((PARTS,)), pltpu.SemaphoreType.DMA((PARTS,)),
        ],
        compiler_params=params(FRAME_MB),
        name="frame_forward",
    )(core, in_hbm(frames), in_hbm(gain), in_hbm(w_up), in_hbm(w_down))


def pieces(value):
    first = value.astype(bf16).astype(f32)
    rest = value - first
    second = rest.astype(bf16).astype(f32)
    return first, second, rest - second


def write_payload(out, mean, top, total):
    lane = lax.broadcasted_iota(jnp.int32, (HALF, 128), 1)
    stats = jnp.zeros((HALF, 128), f32)
    for at, piece in enumerate(pieces(top) + pieces(total)):
        stats = jnp.where(lane == at, piece, stats)
    out[:, :D] = mean.astype(bf16)
    out[:, D:] = stats.astype(bf16)


def read_stats(block):
    stats = block[:, D:].astype(f32)
    lane = lax.broadcasted_iota(jnp.int32, stats.shape, 1)
    top = jnp.sum(jnp.where(lane < 3, stats, 0.0), axis=-1, keepdims=True)
    total = jnp.sum(jnp.where((lane >= 3) & (lane < 6), stats, 0.0), axis=-1, keepdims=True)
    return top, total


def pool_pair(mine, theirs, query, out):
    a = mine[...].astype(f32)
    b = theirs[...].astype(f32)
    q = query[...][None, :]
    score_a = jnp.sum(a * q, axis=-1, keepdims=True) / ROOT
    score_b = jnp.sum(b * q, axis=-1, keepdims=True) / ROOT
    top = jnp.maximum(score_a, score_b)
    weight_a = jnp.exp(score_a - top)
    weight_b = jnp.exp(score_b - top)
    total = weight_a + weight_b
    write_payload(out, (weight_a * a + weight_b * b) / total, top, total)


def pool_all(p0, p1, p2, p3, *rest):
    spread, out = rest[-2:]
    parts = (p0, p1, p2, p3)
    stats = [read_stats(p) for p in parts]
    top = functools.reduce(jnp.maximum, [s[0] for s in stats])
    weights = [jnp.exp(s[0] - top) * s[1] for s in stats]
    total = sum(weights)
    mean = sum(w * p[:, :D].astype(f32) for w, p in zip(weights, parts)) / total
    write_payload(out, mean, top, total)
    rows = mean.astype(bf16)
    for o in range(OWNERS):
        spread[o] = rows


def prepare(
    core, lens, slots, requests, d_encoded, w_out, w_qkv, after,
    d_out, d_attended, own_column, other_column, own_row, other_row, qkv, d_wide, sem,
):
    load = pltpu.make_async_copy(w_qkv, qkv, sem)
    load.start()
    c = core[0]
    lane = lax.broadcasted_iota(jnp.int32, (LP, L), 1)
    diagonal = lane == lax.broadcasted_iota(jnp.int32, (LP, L), 0)
    inside = lax.broadcasted_iota(jnp.int32, (LP, 1), 0) < L
    owner_lane = lax.broadcasted_iota(jnp.int32, (LP, OWNERS), 1)
    cap_lane = lax.broadcasted_iota(jnp.int32, (LP, CAP), 1)
    asked = requests[0].astype(f32).astype(bf16)
    for u in range(USERS):
        slot = jnp.sum(jnp.where(diagonal, slots[u : u + 1, :].astype(f32), 0.0), axis=1, keepdims=True)
        slot = slot.astype(jnp.int32)
        owner = slot >> 6
        lists = dot_nn((owner_lane == owner).astype(bf16), asked)
        local = jnp.sum(jnp.where(cap_lane == (slot & (CAP - 1)), lists, 0.0), axis=1, keepdims=True)
        local = local.astype(jnp.int32)
        position = jnp.where(inside, owner * HALF + (local & (HALF - 1)), -1)
        own = (local >> 6) == c
        here = pl.ds(u * LP, LP)
        own_column[here, :] = jnp.where(own, position, -1)
        other_column[here, :] = jnp.where(own, -1, position)
    square = (128, 128)
    same = lax.broadcasted_iota(jnp.int32, square, 0) == lax.broadcasted_iota(jnp.int32, square, 1)
    for column, row in ((own_column, own_row), (other_column, other_row)):
        for first in range(0, PART, 128):
            for half in range(2):
                size = min(128, PART - first)
                value = column[pl.ds(half * PART + first, size), :].astype(f32)
                if size < 128:
                    value = jnp.concatenate([value, jnp.full((128 - size, 1), -1.0, f32)], axis=0)
                value = jnp.sum(jnp.where(same, value, 0.0), axis=0, keepdims=True)
                row[:, pl.ds(half * LANES + first, 128)] = value.astype(jnp.int32)

    for j in range(D // 128):
        d_wide[j] = d_encoded[:, j * 128 : (j + 1) * 128].astype(f32)
    place = lax.broadcasted_iota(jnp.int32, (LP, 1), 0)
    for first in range(0, USERS, 2):
        pair = []
        for u in (first, first + 1):
            rows = pl.ds(u, L, stride=USERS)
            one = jnp.concatenate([d_wide[j, rows, :] for j in range(D // 128)], axis=1)
            one = jnp.concatenate([one, jnp.zeros((LP - L, D), f32)], axis=0)
            pair.append(jnp.where(place < lens[u], one, 0.0))
        d_out[pl.ds(first * LP, 2 * LP), :] = jnp.concatenate(pair, axis=0).astype(bf16)
    for part in range(USERS // SUB):
        here = pl.ds(part * SUB_ROWS, SUB_ROWS)
        d_attended[here, :] = dot_nt(d_out[here, :], w_out[...]).astype(bf16)
    load.wait()


def run_prepare(core, lens, slots, requests, d_encoded, w_out, w_qkv, after):
    count = USERS * LP
    whole = lambda r, w, t: jax.ShapeDtypeStruct((r, w), t)
    return pl.pallas_call(
        prepare,
        in_specs=[SMEM, SMEM] + [VMEM] * 4 + [HBM, ANY],
        out_specs=[VMEM] * 7,
        out_shape=[
            pltpu.VMEM((count, D), bf16), pltpu.VMEM((count, D), bf16),
            whole(count, 1, jnp.int32), whole(count, 1, jnp.int32),
            whole(1, 2 * LANES, jnp.int32), whole(1, 2 * LANES, jnp.int32), pltpu.VMEM((D, 3 * D), bf16),
        ],
        scratch_shapes=[
            pltpu.VMEM((D // 128, USERS * L, 128), f32), pltpu.SemaphoreType.DMA,
        ],
        compiler_params=params(16),
        cost_estimate=cost(2 * count * D * D, 8 * count * D),
        name="prepare",
    )(core, lens, slots, requests, d_encoded, w_out, in_hbm(w_qkv), after)


def gather(index, table, *rest):
    out = rest[-1]
    at = lax.broadcasted_iota(jnp.int32, (PART, OWNERS * HALF), 1)
    for half in range(2):
        here = pl.ds(half * PART, PART)
        chosen = (at == index[here, :]).astype(bf16)
        out[here, :] = dot_nn(chosen, table[...]).astype(bf16)


def run_gather(index, table, *after):
    count = 2 * PART
    return pl.pallas_call(
        gather,
        in_specs=[VMEM, VMEM] + [ANY] * len(after),
        out_specs=VMEM,
        out_shape=jax.ShapeDtypeStruct((count, D), bf16),
        compiler_params=params(12),
        cost_estimate=cost(2 * count * OWNERS * HALF * D, 6 * count * D),
        name="gather",
    )(index, table, *[in_vmem(x) for x in after])


def encoder(
    lens, index, own_rows, table, pos, gain, w_qkv, w_out, d_out, d_attended, *rest
):
    encoded, d_inputs_a, d_inputs_b = rest[-3:]
    some = ROWS // 2
    at = lax.broadcasted_iota(jnp.int32, (some, OWNERS * HALF), 1)
    places = jnp.concatenate([pos[...].astype(f32), jnp.zeros((LP - L, D), f32)], axis=0)
    g = gain[...][None, :]
    xs, xhats, rstds, packs = [], [], [], []
    for part in range(2):
        here = pl.ds(part * some, some)
        chosen = (at == index[here, :]).astype(bf16)
        x = dot_nn(chosen, table[...]) + own_rows[here, :].astype(f32)
        x = (x.reshape(some // LP, LP, D) + places[None]).reshape(some, D)
        xs.append(x)
    for x in xs:
        xhat, rstd = normalised(x)
        xhats.append(xhat)
        rstds.append(rstd)
        packs.append(dot_nn((xhat * g).astype(bf16), w_qkv[...]).astype(bf16))
    x, xhat, rstd, packed = [jnp.concatenate(v, axis=0) for v in (xs, xhats, rstds, packs)]

    subs = range(GROUP // SUB)
    cut = lambda value, sub: value[sub * SUB_ROWS : (sub + 1) * SUB_ROWS]
    join = lambda values: jnp.concatenate(values, axis=0)
    d_att = d_attended[...]
    q = [cut(packed[:, :D], sub) for sub in subs]
    k = [cut(packed[:, D : 2 * D], sub) for sub in subs]
    v = [cut(packed[:, 2 * D :], sub) for sub in subs]
    place = lax.broadcasted_iota(jnp.int32, (SUB_ROWS, 1), 0)
    column = lax.broadcasted_iota(jnp.int32, (SUB_ROWS, SUB_ROWS), 1)
    raw = [dot_nt(q[sub], k[sub]) for sub in subs]
    d_raw = [dot_nt(cut(d_att, sub), v[sub]) for sub in subs]
    live, probs16, d_scores = [], [], []
    for sub in subs:
        length = jnp.full((SUB_ROWS, 1), 0, jnp.int32)
        first = jnp.full((SUB_ROWS, 1), 0, jnp.int32)
        for u in range(SUB):
            here = (place >= u * LP) & (place < (u + 1) * LP)
            length = jnp.where(here, lens[sub * SUB + u], length)
            first = jnp.where(here, u * LP, first)
        allowed = (column >= first) & (column <= place) & (column < first + length)
        live.append((place - first) < length)
        scores = jnp.where(allowed, raw[sub] / ROOT, MASKED)
        raised = jnp.exp(scores - jnp.max(scores, axis=-1, keepdims=True))
        probs = raised / jnp.sum(raised, axis=-1, keepdims=True)
        probs16.append(probs.astype(bf16))
        d_probs = d_raw[sub].astype(bf16).astype(f32)
        d_scores.append(
            (probs * (d_probs - jnp.sum(d_probs * probs, axis=-1, keepdims=True)) / ROOT).astype(bf16)
        )
    attended = join([dot_nn(probs16[sub], v[sub]).astype(bf16) for sub in subs])
    d_q = join([dot_nn(d_scores[sub], k[sub]).astype(bf16) for sub in subs])
    d_k = join([dot_tn(d_scores[sub], q[sub]).astype(bf16) for sub in subs])
    d_v = join([dot_tn(probs16[sub], cut(d_att, sub)).astype(bf16) for sub in subs])
    encoded[...] = jnp.where(join(live), x + dot_nn(attended, w_out[...]), 0.0).astype(bf16)
    joined = jnp.concatenate([d_q, d_k, d_v], axis=1)
    step_rows = ROWS // 2
    for part in range(2):
        lo, hi = part * step_rows, (part + 1) * step_rows
        d_normed = dot_nt(joined[lo:hi], w_qkv[...]).astype(bf16).astype(f32)
        back = norm_back(d_normed, g, xhat[lo:hi], rstd[lo:hi])
        (d_inputs_a, d_inputs_b)[part][...] = (d_out[lo:hi, :].astype(f32) + back).astype(bf16)


def run_encoder(lens, index, own_rows, table, pos, gain, w_qkv, w_out, d_out, d_attended, early):
    count = USERS * LP
    return pl.pallas_call(
        encoder,
        in_specs=[
            SMEM, VMEM, VMEM, VMEM, VMEM, VMEM, VMEM, VMEM, VMEM, VMEM, *[ANY] * len(early),
        ],
        out_specs=[VMEM] * 3,
        out_shape=[jax.ShapeDtypeStruct((rows, D), bf16) for rows in (count, PART, PART)],
        compiler_params=params(ENC_MB),
        name="user_encoder",
    )(lens, index, own_rows, table, pos, gain, in_vmem(w_qkv), w_out, in_vmem(d_out), in_vmem(d_attended), *[in_vmem(x) for x in early])


def reorder(by_user, after, by_place, wide):
    for first in range(0, USERS, 2):
        pair = by_user[pl.ds(first * LP, 2 * LP), :].astype(f32)
        for k in range(2):
            for j in range(D // 128):
                one = pair[k * LP : k * LP + L, j * 128 : (j + 1) * 128]
                wide[j, pl.ds(first + k, L, stride=USERS), :] = one
    for j in range(D // 128):
        by_place[:, j * 128 : (j + 1) * 128] = wide[j].astype(bf16)


def run_reorder(by_user, after):
    return pl.pallas_call(
        reorder,
        in_specs=[VMEM, ANY],
        out_specs=VMEM,
        out_shape=jax.ShapeDtypeStruct((USERS * L, D), bf16),
        scratch_shapes=[pltpu.VMEM((D // 128, USERS * L, 128), f32)],
        compiler_params=params(12),
        cost_estimate=cost(USERS * L * D, 6 * USERS * L * D),
        name="reorder",
    )(by_user, after)


def add_owners(parts, out):
    total = parts[0].astype(f32)
    for o in range(1, OWNERS):
        total = total + parts[o].astype(f32)
    out[...] = total.astype(bf16)


def add_parts(a, b, c, d, after, out):
    out[...] = sum(part[...].astype(f32) for part in (a, b, c, d)).astype(bf16)


def scatter(halves, own, index, *operands):
    out = operands[-1]
    rows = operands[: len(halves)]
    block = OWNERS * HALF // 2
    for k in range(2):
        here = pl.ds(k * block, block)
        row = lax.broadcasted_iota(jnp.int32, (block, PART), 0) + k * block
        total = None if own else operands[len(halves)][here, :].astype(f32)
        for half, part in zip(halves, rows):
            chosen = (row == index[:, pl.ds(half * LANES, PART)]).astype(bf16)
            more = dot_nn(chosen, part[...])
            total = more if total is None else total + more
        out[here, :] = total.astype(bf16)


def run_scatter(halves, own, *operands):
    count = PART * len(halves)
    return pl.pallas_call(
        functools.partial(scatter, halves, own),
        in_specs=[VMEM] * len(operands),
        out_specs=VMEM,
        out_shape=jax.ShapeDtypeStruct((OWNERS * HALF, D), bf16),
        compiler_params=params(12),
        cost_estimate=cost(2 * count * OWNERS * HALF * D, 6 * count * D),
        name="scatter",
    )(*operands)


def turn(up, down, after, up_t, down_t):
    for p in range(PARTS):
        cut = pl.ds(p * (HID // PARTS), HID // PARTS)
        up_t[cut, :] = up[:, cut].T
        down_t[:, cut] = down[cut, :].T


def run_turn(up, down, after):
    return pl.pallas_call(
        turn,
        in_specs=[VMEM, VMEM, ANY],
        out_specs=[VMEM] * 2,
        out_shape=[pltpu.VMEM((HID, D), bf16), pltpu.VMEM((D, HID), bf16)],
        compiler_params=params(8),
        cost_estimate=cost(HID * D, 8 * HID * D),
        name="turn",
    )(in_vmem(up), in_vmem(down), after)


def frame_backward(
    core, d_mine, d_other, pay_mine, pay_other, query, frames, framed, gain, slope, up, down,
    out,
):
    upper = core[0] == 1
    order = lambda a, b: jnp.concatenate([jnp.where(upper, b, a), jnp.where(upper, a, b)], axis=0)
    dp = order(d_mine[...], d_other[...]).astype(f32)
    pay = order(pay_mine[...], pay_other[...]).astype(f32)
    x = framed[...].astype(f32)
    q = query[...][None, :]
    top, whole = read_stats(pay)
    weight = jnp.exp(jnp.sum(x * q, axis=-1, keepdims=True) / ROOT - top) / whole
    cross = jnp.sum(dp * x, axis=-1, keepdims=True)
    own = jnp.sum(dp * pay[:, :D], axis=-1, keepdims=True)
    grad = weight * (dp + ((cross - own) / ROOT) * q)
    grad16 = grad.astype(bf16)
    width = HID // PARTS
    total = jnp.zeros(grad.shape, f32)
    for p in range(PARTS):
        cut = pl.ds(p * width, width)
        d_hidden = dot_nn(grad16, down[:, cut]).astype(bf16).astype(f32)
        d_a = (d_hidden * slope[:, cut].astype(f32)).astype(bf16)
        total = total + dot_nn(d_a, up[cut, :])
    xhat, rstd = normalised(frames[...].astype(f32))
    d_normed = total.astype(bf16).astype(f32)
    out[...] = (grad + norm_back(d_normed, gain[...][None, :], xhat, rstd)).astype(bf16)


def run_frame_backward(core, d_mine, d_other, pay_mine, pay_other, query, frames, framed, gain, slope, w_up, w_down):
    rows = frames.shape[0]
    return pl.pallas_call(
        frame_backward,
        in_specs=[SMEM] + [VMEM] * 11,
        out_specs=VMEM,
        out_shape=jax.ShapeDtypeStruct((rows, D), bf16),
        compiler_params=params(FRAME_MB),
        name="frame_backward",
    )(core, d_mine, d_other, pay_mine, pay_other, query, frames, framed, gain, slope, in_vmem(w_up), in_vmem(w_down))


def swap_with(x, bits):
    pairs = [(i, i ^ bits) for i in range(8)]
    return lax.ppermute(x, "frame", pairs)


def spread_along_x(x):
    return [swap_with(x, 2 * k) for k in (1, 2, 3)]


def shards(
    frames, frame_gain, w_up, w_down, pool_query, pos_embed, user_gain, w_qkv, w_out,
    request_rows, hist_slot, hist_len, d_encoded,
):
    rows = frames.shape[0]
    c = lax.axis_index("frame") % 2
    core = c.astype(jnp.int32).reshape(1)
    flat_frames = frames.reshape(rows, D)
    gain = frame_gain
    query = pool_query

    mine, other, framed, slope, up, down = run_frame_forward(core, flat_frames, gain, w_up, w_down)
    theirs = swap_with(other, 1)
    payload = jax.ShapeDtypeStruct((HALF, PAY), bf16)
    pair = pl.pallas_call(
        pool_pair, in_specs=[VMEM] * 3, out_specs=VMEM, out_shape=payload, compiler_params=params(8), name="pool_pair",
    )(mine, theirs, query)
    cotangent = jnp.transpose(d_encoded, (1, 0, 2)).reshape(USERS * L, D)
    d_out, d_attended, own_column, other_column, own_row, other_row, qkv = run_prepare(
        core, hist_len, hist_slot, request_rows, cotangent, w_out, w_qkv, pair
    )
    up_turned, down_turned = run_turn(up, down, pair)
    early = (in_vmem(d_out), in_vmem(up_turned))
    spread, pay_mine = pl.pallas_call(
        pool_all, in_specs=[VMEM] * 4 + [pl.BlockSpec(memory_space=pl.ANY)] * len(early), out_specs=[VMEM] * 2,
        out_shape=[jax.ShapeDtypeStruct((OWNERS, HALF, D), bf16), payload], compiler_params=params(8), name="pool_all",
    )(pair, *spread_along_x(pair), *early)
    table = lax.all_to_all(spread, "dp", split_axis=0, concat_axis=0, tiled=True).reshape(OWNERS * HALF, D)
    other_table = swap_with(table, 1)
    own_rows = run_gather(own_column, table)
    peer_index = swap_with(other_row, 1)
    pay_other = swap_with(pay_mine, 1)
    encoded, d_a, d_b = run_encoder(
        hist_len, other_column, own_rows, other_table, pos_embed, user_gain, qkv, w_out, d_out, d_attended,
        (peer_index, pay_other),
    )
    back_a = swap_with(d_a, 1)
    back_b = swap_with(d_b, 1)
    d_table = run_scatter((0, 1), True, own_row, d_a, d_b)
    d_table = run_scatter((0,), False, peer_index, back_a, d_table)
    d_table = run_scatter((1,), False, peer_index, back_b, d_table)
    returned = lax.all_to_all(
        d_table.reshape(OWNERS, HALF, D), "dp", split_axis=0, concat_axis=0, tiled=True
    )
    partial = pl.pallas_call(
        add_owners, in_specs=[VMEM], out_specs=VMEM, out_shape=jax.ShapeDtypeStruct((HALF, D), bf16),
        compiler_params=params(8), name="add_owners",
    )(returned)
    encoded = run_reorder(encoded, partial)
    d_mine = pl.pallas_call(
        add_parts, in_specs=[VMEM] * 4 + [ANY], out_specs=VMEM, out_shape=jax.ShapeDtypeStruct((HALF, D), bf16),
        compiler_params=params(8), name="add_parts",
    )(partial, *spread_along_x(partial), in_hbm(encoded))
    d_other = swap_with(d_mine, 1)
    d_frames = run_frame_backward(
        core, d_mine, d_other, pay_mine, pay_other, query, flat_frames, framed, gain, slope, up_turned, down_turned
    )
    encoded = jnp.transpose(encoded.reshape(L, USERS, D), (1, 0, 2))
    return encoded, d_frames.reshape(rows, 1, D)


def solution(mesh):
    in_specs = (
        P("dp", "frame", None),
        P(),
        P(),
        P(),
        P(),
        P(),
        P(),
        P(),
        P(),
        P(("dp", "frame"), None, None),
        P(("dp", "frame"), None),
        P(("dp", "frame")),
        P(("dp", "frame"), None, None),
    )
    out_specs = (P(("dp", "frame"), None, None), P("dp", "frame", None))
    return jax.shard_map(shards, mesh=mesh, in_specs=in_specs, out_specs=out_specs, check_vma=False)
```

```python
import functools
import math

import jax
import jax.numpy as jnp
from jax import lax
from jax.experimental import pallas as pl
from jax.experimental.pallas import tpu as pltpu
from jax.sharding import PartitionSpec as P

D = 768
HID = 3072
L = 50
LP = 56
USERS = 16
GROUP = 16
ROWS = GROUP * LP
SUB = 4
SUB_ROWS = SUB * LP
ENC_MB = 36
PART = USERS * LP // 2
LANES = 512
OWNERS = 16
HALF = 64
CAP = 64
PAY = D + 128
EPS = 1e-6
ROOT = math.sqrt(D)
MASKED = -1e9
AXES = ("dp", "frame")
f32 = jnp.float32
bf16 = jnp.bfloat16
VMEM = pl.BlockSpec(memory_space=pltpu.VMEM)
SMEM = pl.BlockSpec(memory_space=pltpu.SMEM)
ANY = pl.BlockSpec(memory_space=pl.ANY)
HBM = pl.BlockSpec(memory_space=pltpu.HBM)
PARTS = 4
FRAME_MB = 16


def dot_nn(a, b):
    return lax.dot_general(a, b, (((1,), (0,)), ((), ())), preferred_element_type=f32)


def dot_nt(a, b):
    return lax.dot_general(a, b, (((1,), (1,)), ((), ())), preferred_element_type=f32)


def dot_tn(a, b):
    return lax.dot_general(a, b, (((0,), (0,)), ((), ())), preferred_element_type=f32)


def in_vmem(x):
    return pltpu.with_memory_space_constraint(x, pltpu.VMEM)


def in_hbm(x):
    return pltpu.with_memory_space_constraint(x, pltpu.HBM)


def params(megabytes):
    return pltpu.CompilerParams(vmem_limit_bytes=megabytes << 20)


def cost(flops, moved):
    return pl.CostEstimate(flops=int(flops), bytes_accessed=int(moved), transcendentals=0)


def normalised(x):
    centred = x - jnp.mean(x, axis=-1, keepdims=True)
    rstd = lax.rsqrt(jnp.mean(centred * centred, axis=-1, keepdims=True) + EPS)
    return centred * rstd, rstd


def norm_back(d_normed, gain, xhat, rstd):
    d_hat = d_normed * gain
    along = jnp.mean(d_hat * xhat, axis=-1, keepdims=True)
    return rstd * (d_hat - jnp.mean(d_hat, axis=-1, keepdims=True) - xhat * along)


def fetch(source, target, sems, axis, parts):
    width = source.shape[axis] // parts
    copies = []
    for p in range(parts):
        cut = pl.ds(p * width, width)
        where = (cut, slice(None)) if axis == 0 else (slice(None), cut)
        copies.append(pltpu.make_async_copy(source.at[where], target.at[where], sems.at[p]))
    return copies


def frame_forward(
    core, frames_in, gain_in, w_up, w_down, mine, other, out, slope, up, down, frames, gain, sems, up_sems, down_sems
):
    first = [pltpu.make_async_copy(frames_in, frames, sems.at[0]), pltpu.make_async_copy(gain_in, gain, sems.at[1])]
    for one in first:
        one.start()
    ups = fetch(w_up, up, up_sems, 1, PARTS)
    downs = fetch(w_down, down, down_sems, 0, PARTS)
    for one, two in zip(ups, downs):
        one.start()
        two.start(priority=1)
    for one in first:
        one.wait()
    x = frames[...].astype(f32)
    xhat, _ = normalised(x)
    normed = (xhat * gain[...][None, :]).astype(bf16)
    total = x
    width = HID // PARTS
    c0 = math.sqrt(2.0 / math.pi)
    for p in range(PARTS):
        cut = pl.ds(p * width, width)
        ups[p].wait()
        a = dot_nn(normed, up[:, cut])
        square = a * a
        th = jnp.tanh(c0 * a * (1.0 + 0.044715 * square))
        half = 0.5 * (1.0 + th)
        hidden = (a * half).astype(bf16)
        slope[:, cut] = (half + 0.5 * a * (1.0 - th * th) * c0 * (1.0 + 3 * 0.044715 * square)).astype(bf16)
        downs[p].wait()
        total = total + dot_nn(hidden, down[cut, :])
    stored = total.astype(bf16)
    out[...] = stored
    upper = core[0] == 1
    mine[...] = jnp.where(upper, stored[HALF:], stored[:HALF])
    other[...] = jnp.where(upper, stored[:HALF], stored[HALF:])


def run_frame_forward(core, frames, gain, w_up, w_down):
    rows = frames.shape[0]
    return pl.pallas_call(
        frame_forward,
        in_specs=[SMEM, HBM, HBM, HBM, HBM],
        out_specs=[VMEM] * 6,
        out_shape=[
            jax.ShapeDtypeStruct((HALF, D), bf16),
            jax.ShapeDtypeStruct((HALF, D), bf16),
            jax.ShapeDtypeStruct((rows, D), bf16),
            jax.ShapeDtypeStruct((rows, HID), bf16),
            pltpu.VMEM((D, HID), bf16),
            pltpu.VMEM((HID, D), bf16),
        ],
        scratch_shapes=[
            pltpu.VMEM((rows, D), bf16), pltpu.VMEM((D,), f32), pltpu.SemaphoreType.DMA((2,)),
            pltpu.SemaphoreType.DMA((PARTS,)), pltpu.SemaphoreType.DMA((PARTS,)),
        ],
        compiler_params=params(FRAME_MB),
        name="frame_forward",
    )(core, in_hbm(frames), in_hbm(gain), in_hbm(w_up), in_hbm(w_down))


def pieces(value):
    first = value.astype(bf16).astype(f32)
    rest = value - first
    second = rest.astype(bf16).astype(f32)
    return first, second, rest - second


def write_payload(out, mean, top, total):
    lane = lax.broadcasted_iota(jnp.int32, (HALF, 128), 1)
    stats = jnp.zeros((HALF, 128), f32)
    for at, piece in enumerate(pieces(top) + pieces(total)):
        stats = jnp.where(lane == at, piece, stats)
    out[:, :D] = mean.astype(bf16)
    out[:, D:] = stats.astype(bf16)


def read_stats(block):
    stats = block[:, D:].astype(f32)
    lane = lax.broadcasted_iota(jnp.int32, stats.shape, 1)
    top = jnp.sum(jnp.where(lane < 3, stats, 0.0), axis=-1, keepdims=True)
    total = jnp.sum(jnp.where((lane >= 3) & (lane < 6), stats, 0.0), axis=-1, keepdims=True)
    return top, total


def pool_pair(mine, theirs, query, out):
    a = mine[...].astype(f32)
    b = theirs[...].astype(f32)
    q = query[...][None, :]
    score_a = jnp.sum(a * q, axis=-1, keepdims=True) / ROOT
    score_b = jnp.sum(b * q, axis=-1, keepdims=True) / ROOT
    top = jnp.maximum(score_a, score_b)
    weight_a = jnp.exp(score_a - top)
    weight_b = jnp.exp(score_b - top)
    total = weight_a + weight_b
    write_payload(out, (weight_a * a + weight_b * b) / total, top, total)


def pool_all(p0, p1, p2, p3, *rest):
    spread, out = rest[-2:]
    parts = (p0, p1, p2, p3)
    stats = [read_stats(p) for p in parts]
    top = functools.reduce(jnp.maximum, [s[0] for s in stats])
    weights = [jnp.exp(s[0] - top) * s[1] for s in stats]
    total = sum(weights)
    mean = sum(w * p[:, :D].astype(f32) for w, p in zip(weights, parts)) / total
    write_payload(out, mean, top, total)
    rows = mean.astype(bf16)
    for o in range(OWNERS):
        spread[o] = rows


def prepare(
    core, lens, slots, requests, d_encoded, w_out, w_qkv, after,
    d_out, d_attended, own_column, other_column, own_row, other_row, qkv, d_wide, sem,
):
    load = pltpu.make_async_copy(w_qkv, qkv, sem)
    load.start()
    c = core[0]
    lane = lax.broadcasted_iota(jnp.int32, (LP, L), 1)
    diagonal = lane == lax.broadcasted_iota(jnp.int32, (LP, L), 0)
    inside = lax.broadcasted_iota(jnp.int32, (LP, 1), 0) < L
    owner_lane = lax.broadcasted_iota(jnp.int32, (LP, OWNERS), 1)
    cap_lane = lax.broadcasted_iota(jnp.int32, (LP, CAP), 1)
    asked = requests[0].astype(f32).astype(bf16)
    for u in range(USERS):
        slot = jnp.sum(jnp.where(diagonal, slots[u : u + 1, :].astype(f32), 0.0), axis=1, keepdims=True)
        slot = slot.astype(jnp.int32)
        owner = slot >> 6
        lists = dot_nn((owner_lane == owner).astype(bf16), asked)
        local = jnp.sum(jnp.where(cap_lane == (slot & (CAP - 1)), lists, 0.0), axis=1, keepdims=True)
        local = local.astype(jnp.int32)
        position = jnp.where(inside, owner * HALF + (local & (HALF - 1)), -1)
        own = (local >> 6) == c
        here = pl.ds(u * LP, LP)
        own_column[here, :] = jnp.where(own, position, -1)
        other_column[here, :] = jnp.where(own, -1, position)
    square = (128, 128)
    same = lax.broadcasted_iota(jnp.int32, square, 0) == lax.broadcasted_iota(jnp.int32, square, 1)
    for column, row in ((own_column, own_row), (other_column, other_row)):
        for first in range(0, PART, 128):
            for half in range(2):
                size = min(128, PART - first)
                value = column[pl.ds(half * PART + first, size), :].astype(f32)
                if size < 128:
                    value = jnp.concatenate([value, jnp.full((128 - size, 1), -1.0, f32)], axis=0)
                value = jnp.sum(jnp.where(same, value, 0.0), axis=0, keepdims=True)
                row[:, pl.ds(half * LANES + first, 128)] = value.astype(jnp.int32)

    for j in range(D // 128):
        d_wide[j] = d_encoded[:, j * 128 : (j + 1) * 128].astype(f32)
    place = lax.broadcasted_iota(jnp.int32, (LP, 1), 0)
    for first in range(0, USERS, 2):
        pair = []
        for u in (first, first + 1):
            rows = pl.ds(u, L, stride=USERS)
            one = jnp.concatenate([d_wide[j, rows, :] for j in range(D // 128)], axis=1)
            one = jnp.concatenate([one, jnp.zeros((LP - L, D), f32)], axis=0)
            pair.append(jnp.where(place < lens[u], one, 0.0))
        d_out[pl.ds(first * LP, 2 * LP), :] = jnp.concatenate(pair, axis=0).astype(bf16)
    for part in range(USERS // SUB):
        here = pl.ds(part * SUB_ROWS, SUB_ROWS)
        d_attended[here, :] = dot_nt(d_out[here, :], w_out[...]).astype(bf16)
    load.wait()


def run_prepare(core, lens, slots, requests, d_encoded, w_out, w_qkv, after):
    count = USERS * LP
    whole = lambda r, w, t: jax.ShapeDtypeStruct((r, w), t)
    return pl.pallas_call(
        prepare,
        in_specs=[SMEM, SMEM] + [VMEM] * 4 + [HBM, ANY],
        out_specs=[VMEM] * 7,
        out_shape=[
            pltpu.VMEM((count, D), bf16), pltpu.VMEM((count, D), bf16),
            whole(count, 1, jnp.int32), whole(count, 1, jnp.int32),
            whole(1, 2 * LANES, jnp.int32), whole(1, 2 * LANES, jnp.int32), pltpu.VMEM((D, 3 * D), bf16),
        ],
        scratch_shapes=[
            pltpu.VMEM((D // 128, USERS * L, 128), f32), pltpu.SemaphoreType.DMA,
        ],
        compiler_params=params(16),
        cost_estimate=cost(2 * count * D * D, 8 * count * D),
        name="prepare",
    )(core, lens, slots, requests, d_encoded, w_out, in_hbm(w_qkv), after)


def gather(index, table, *rest):
    out = rest[-1]
    at = lax.broadcasted_iota(jnp.int32, (PART, OWNERS * HALF), 1)
    for half in range(2):
        here = pl.ds(half * PART, PART)
        chosen = (at == index[here, :]).astype(bf16)
        out[here, :] = dot_nn(chosen, table[...]).astype(bf16)


def run_gather(index, table, *after):
    count = 2 * PART
    return pl.pallas_call(
        gather,
        in_specs=[VMEM, VMEM] + [ANY] * len(after),
        out_specs=VMEM,
        out_shape=jax.ShapeDtypeStruct((count, D), bf16),
        compiler_params=params(12),
        cost_estimate=cost(2 * count * OWNERS * HALF * D, 6 * count * D),
        name="gather",
    )(index, table, *[in_vmem(x) for x in after])


def encoder(
    lens, index, own_rows, table, pos, gain, w_qkv, w_out, d_out, d_attended, *rest
):
    encoded, d_inputs_a, d_inputs_b = rest[-3:]
    some = ROWS // 2
    at = lax.broadcasted_iota(jnp.int32, (some, OWNERS * HALF), 1)
    places = jnp.concatenate([pos[...].astype(f32), jnp.zeros((LP - L, D), f32)], axis=0)
    g = gain[...][None, :]
    xs, xhats, rstds, packs = [], [], [], []
    for part in range(2):
        here = pl.ds(part * some, some)
        chosen = (at == index[here, :]).astype(bf16)
        x = dot_nn(chosen, table[...]) + own_rows[here, :].astype(f32)
        x = (x.reshape(some // LP, LP, D) + places[None]).reshape(some, D)
        xs.append(x)
    for x in xs:
        xhat, rstd = normalised(x)
        xhats.append(xhat)
        rstds.append(rstd)
        packs.append(dot_nn((xhat * g).astype(bf16), w_qkv[...]).astype(bf16))
    x, xhat, rstd, packed = [jnp.concatenate(v, axis=0) for v in (xs, xhats, rstds, packs)]

    subs = range(GROUP // SUB)
    cut = lambda value, sub: value[sub * SUB_ROWS : (sub + 1) * SUB_ROWS]
    join = lambda values: jnp.concatenate(values, axis=0)
    d_att = d_attended[...]
    q = [cut(packed[:, :D], sub) for sub in subs]
    k = [cut(packed[:, D : 2 * D], sub) for sub in subs]
    v = [cut(packed[:, 2 * D :], sub) for sub in subs]
    place = lax.broadcasted_iota(jnp.int32, (SUB_ROWS, 1), 0)
    column = lax.broadcasted_iota(jnp.int32, (SUB_ROWS, SUB_ROWS), 1)
    raw = [dot_nt(q[sub], k[sub]) for sub in subs]
    d_raw = [dot_nt(cut(d_att, sub), v[sub]) for sub in subs]
    live, probs16, d_scores = [], [], []
    for sub in subs:
        length = jnp.full((SUB_ROWS, 1), 0, jnp.int32)
        first = jnp.full((SUB_ROWS, 1), 0, jnp.int32)
        for u in range(SUB):
            here = (place >= u * LP) & (place < (u + 1) * LP)
            length = jnp.where(here, lens[sub * SUB + u], length)
            first = jnp.where(here, u * LP, first)
        allowed = (column >= first) & (column <= place) & (column < first + length)
        live.append((place - first) < length)
        scores = jnp.where(allowed, raw[sub] / ROOT, MASKED)
        raised = jnp.exp(scores - jnp.max(scores, axis=-1, keepdims=True))
        probs = raised / jnp.sum(raised, axis=-1, keepdims=True)
        probs16.append(probs.astype(bf16))
        d_probs = d_raw[sub].astype(bf16).astype(f32)
        d_scores.append(
            (probs * (d_probs - jnp.sum(d_probs * probs, axis=-1, keepdims=True)) / ROOT).astype(bf16)
        )
    attended = join([dot_nn(probs16[sub], v[sub]).astype(bf16) for sub in subs])
    d_q = join([dot_nn(d_scores[sub], k[sub]).astype(bf16) for sub in subs])
    d_k = join([dot_tn(d_scores[sub], q[sub]).astype(bf16) for sub in subs])
    d_v = join([dot_tn(probs16[sub], cut(d_att, sub)).astype(bf16) for sub in subs])
    encoded[...] = jnp.where(join(live), x + dot_nn(attended, w_out[...]), 0.0).astype(bf16)
    joined = jnp.concatenate([d_q, d_k, d_v], axis=1)
    step_rows = ROWS // 2
    for part in range(2):
        lo, hi = part * step_rows, (part + 1) * step_rows
        d_normed = dot_nt(joined[lo:hi], w_qkv[...]).astype(bf16).astype(f32)
        back = norm_back(d_normed, g, xhat[lo:hi], rstd[lo:hi])
        (d_inputs_a, d_inputs_b)[part][...] = (d_out[lo:hi, :].astype(f32) + back).astype(bf16)


def run_encoder(lens, index, own_rows, table, pos, gain, w_qkv, w_out, d_out, d_attended, early):
    count = USERS * LP
    return pl.pallas_call(
        encoder,
        in_specs=[
            SMEM, VMEM, VMEM, VMEM, VMEM, VMEM, VMEM, VMEM, VMEM, VMEM, *[ANY] * len(early),
        ],
        out_specs=[VMEM] * 3,
        out_shape=[jax.ShapeDtypeStruct((rows, D), bf16) for rows in (count, PART, PART)],
        compiler_params=params(ENC_MB),
        name="user_encoder",
    )(lens, index, own_rows, table, pos, gain, in_vmem(w_qkv), w_out, in_vmem(d_out), in_vmem(d_attended), *[in_vmem(x) for x in early])


def reorder(by_user, after, by_place, wide):
    for first in range(0, USERS, 2):
        pair = by_user[pl.ds(first * LP, 2 * LP), :].astype(f32)
        for k in range(2):
            for j in range(D // 128):
                one = pair[k * LP : k * LP + L, j * 128 : (j + 1) * 128]
                wide[j, pl.ds(first + k, L, stride=USERS), :] = one
    for j in range(D // 128):
        by_place[:, j * 128 : (j + 1) * 128] = wide[j].astype(bf16)


def run_reorder(by_user, after):
    return pl.pallas_call(
        reorder,
        in_specs=[VMEM, ANY],
        out_specs=VMEM,
        out_shape=jax.ShapeDtypeStruct((USERS * L, D), bf16),
        scratch_shapes=[pltpu.VMEM((D // 128, USERS * L, 128), f32)],
        compiler_params=params(12),
        cost_estimate=cost(USERS * L * D, 6 * USERS * L * D),
        name="reorder",
    )(by_user, after)


def add_owners(parts, out):
    total = parts[0].astype(f32)
    for o in range(1, OWNERS):
        total = total + parts[o].astype(f32)
    out[...] = total.astype(bf16)


def add_parts(a, b, c, d, after, out):
    out[...] = sum(part[...].astype(f32) for part in (a, b, c, d)).astype(bf16)


def scatter(halves, own, index, *operands):
    out = operands[-1]
    rows = operands[: len(halves)]
    block = OWNERS * HALF // 2
    for k in range(2):
        here = pl.ds(k * block, block)
        row = lax.broadcasted_iota(jnp.int32, (block, PART), 0) + k * block
        total = None if own else operands[len(halves)][here, :].astype(f32)
        for half, part in zip(halves, rows):
            chosen = (row == index[:, pl.ds(half * LANES, PART)]).astype(bf16)
            more = dot_nn(chosen, part[...])
            total = more if total is None else total + more
        out[here, :] = total.astype(bf16)


def run_scatter(halves, own, *operands):
    count = PART * len(halves)
    return pl.pallas_call(
        functools.partial(scatter, halves, own),
        in_specs=[VMEM] * len(operands),
        out_specs=VMEM,
        out_shape=jax.ShapeDtypeStruct((OWNERS * HALF, D), bf16),
        compiler_params=params(12),
        cost_estimate=cost(2 * count * OWNERS * HALF * D, 6 * count * D),
        name="scatter",
    )(*operands)


def turn(up, down, after, up_t, down_t):
    for p in range(PARTS):
        cut = pl.ds(p * (HID // PARTS), HID // PARTS)
        up_t[cut, :] = up[:, cut].T
        down_t[:, cut] = down[cut, :].T


def run_turn(up, down, after):
    return pl.pallas_call(
        turn,
        in_specs=[VMEM, VMEM, ANY],
        out_specs=[VMEM] * 2,
        out_shape=[pltpu.VMEM((HID, D), bf16), pltpu.VMEM((D, HID), bf16)],
        compiler_params=params(8),
        cost_estimate=cost(HID * D, 8 * HID * D),
        name="turn",
    )(in_vmem(up), in_vmem(down), after)


def frame_backward(
    core, d_mine, d_other, pay_mine, pay_other, query, frames, framed, gain, slope, up, down,
    out,
):
    upper = core[0] == 1
    order = lambda a, b: jnp.concatenate([jnp.where(upper, b, a), jnp.where(upper, a, b)], axis=0)
    dp = order(d_mine[...], d_other[...]).astype(f32)
    pay = order(pay_mine[...], pay_other[...]).astype(f32)
    x = framed[...].astype(f32)
    q = query[...][None, :]
    top, whole = read_stats(pay)
    weight = jnp.exp(jnp.sum(x * q, axis=-1, keepdims=True) / ROOT - top) / whole
    cross = jnp.sum(dp * x, axis=-1, keepdims=True)
    own = jnp.sum(dp * pay[:, :D], axis=-1, keepdims=True)
    grad = weight * (dp + ((cross - own) / ROOT) * q)
    grad16 = grad.astype(bf16)
    width = HID // PARTS
    total = jnp.zeros(grad.shape, f32)
    for p in range(PARTS):
        cut = pl.ds(p * width, width)
        d_hidden = dot_nn(grad16, down[:, cut]).astype(bf16).astype(f32)
        d_a = (d_hidden * slope[:, cut].astype(f32)).astype(bf16)
        total = total + dot_nn(d_a, up[cut, :])
    xhat, rstd = normalised(frames[...].astype(f32))
    d_normed = total.astype(bf16).astype(f32)
    out[...] = (grad + norm_back(d_normed, gain[...][None, :], xhat, rstd)).astype(bf16)


def run_frame_backward(core, d_mine, d_other, pay_mine, pay_other, query, frames, framed, gain, slope, w_up, w_down):
    rows = frames.shape[0]
    return pl.pallas_call(
        frame_backward,
        in_specs=[SMEM] + [VMEM] * 11,
        out_specs=VMEM,
        out_shape=jax.ShapeDtypeStruct((rows, D), bf16),
        compiler_params=params(FRAME_MB),
        name="frame_backward",
    )(core, d_mine, d_other, pay_mine, pay_other, query, frames, framed, gain, slope, in_vmem(w_up), in_vmem(w_down))


def swap_with(x, bits):
    pairs = [(i, i ^ bits) for i in range(8)]
    return lax.ppermute(x, "frame", pairs)


def spread_along_x(x):
    return [swap_with(x, 2 * k) for k in (1, 2, 3)]


def shards(
    frames, frame_gain, w_up, w_down, pool_query, pos_embed, user_gain, w_qkv, w_out,
    request_rows, hist_slot, hist_len, d_encoded,
):
    rows = frames.shape[0]
    c = lax.axis_index("frame") % 2
    core = c.astype(jnp.int32).reshape(1)
    flat_frames = frames.reshape(rows, D)
    gain = frame_gain
    query = pool_query

    mine, other, framed, slope, up, down = run_frame_forward(core, flat_frames, gain, w_up, w_down)
    theirs = swap_with(other, 1)
    payload = jax.ShapeDtypeStruct((HALF, PAY), bf16)
    pair = pl.pallas_call(
        pool_pair, in_specs=[VMEM] * 3, out_specs=VMEM, out_shape=payload, compiler_params=params(8), name="pool_pair",
    )(mine, theirs, query)
    cotangent = jnp.transpose(d_encoded, (1, 0, 2)).reshape(USERS * L, D)
    d_out, d_attended, own_column, other_column, own_row, other_row, qkv = run_prepare(
        core, hist_len, hist_slot, request_rows, cotangent, w_out, w_qkv, pair
    )
    up_turned, down_turned = run_turn(up, down, pair)
    early = (in_vmem(d_out), in_vmem(up_turned))
    spread, pay_mine = pl.pallas_call(
        pool_all, in_specs=[VMEM] * 4 + [pl.BlockSpec(memory_space=pl.ANY)] * len(early), out_specs=[VMEM] * 2,
        out_shape=[jax.ShapeDtypeStruct((OWNERS, HALF, D), bf16), payload], compiler_params=params(8), name="pool_all",
    )(pair, *spread_along_x(pair), *early)
    table = lax.all_to_all(spread, "dp", split_axis=0, concat_axis=0, tiled=True).reshape(OWNERS * HALF, D)
    other_table = swap_with(table, 1)
    own_rows = run_gather(own_column, table)
    peer_index = swap_with(other_row, 1)
    pay_other = swap_with(pay_mine, 1)
    encoded, d_a, d_b = run_encoder(
        hist_len, other_column, own_rows, other_table, pos_embed, user_gain, qkv, w_out, d_out, d_attended,
        (peer_index, pay_other),
    )
    back_a = swap_with(d_a, 1)
    back_b = swap_with(d_b, 1)
    d_table = run_scatter((0, 1), True, own_row, d_a, d_b)
    d_table = run_scatter((0,), False, peer_index, back_a, d_table)
    d_table = run_scatter((1,), False, peer_index, back_b, d_table)
    returned = lax.all_to_all(
        d_table.reshape(OWNERS, HALF, D), "dp", split_axis=0, concat_axis=0, tiled=True
    )
    partial = pl.pallas_call(
        add_owners, in_specs=[VMEM], out_specs=VMEM, out_shape=jax.ShapeDtypeStruct((HALF, D), bf16),
        compiler_params=params(8), name="add_owners",
    )(returned)
    encoded = run_reorder(encoded, partial)
    d_mine = pl.pallas_call(
        add_parts, in_specs=[VMEM] * 4 + [ANY], out_specs=VMEM, out_shape=jax.ShapeDtypeStruct((HALF, D), bf16),
        compiler_params=params(8), name="add_parts",
    )(partial, *spread_along_x(partial), in_hbm(encoded))
    d_other = swap_with(d_mine, 1)
    d_frames = run_frame_backward(
        core, d_mine, d_other, pay_mine, pay_other, query, flat_frames, framed, gain, slope, up_turned, down_turned
    )
    encoded = jnp.transpose(encoded.reshape(L, USERS, D), (1, 0, 2))
    return encoded, d_frames.reshape(rows, 1, D)


def solution(mesh):
    in_specs = (
        P("dp", "frame", None),
        P(),
        P(),
        P(),
        P(),
        P(),
        P(),
        P(),
        P(),
        P(("dp", "frame"), None, None),
        P(("dp", "frame"), None),
        P(("dp", "frame")),
        P(("dp", "frame"), None, None),
    )
    out_specs = (P(("dp", "frame"), None, None), P("dp", "frame", None))
    return jax.shard_map(shards, mesh=mesh, in_specs=in_specs, out_specs=out_specs, check_vma=False)
```
